256 devices in a mesh: gx: 32 (over z, y_lo, core), gy: 2 (over y_hi), gz: 4 (over x).
Axes of the slice: x: 4, y: 4 (y_hi: 2, y_lo: 2; y = y_hi * 2 + y_lo), z: 8, core: 2. Of those that a mesh axis runs over, the one named last changes fastest.
Arguments:
- jacobian: bfloat16 [32, 8, 12, 64, 1728], P('gx', 'gy', 'gz'), may hold values from -0.06 to 1.06
- columns: int32 [32, 8, 12, 27], P('gx', 'gy', 'gz'), may hold values from 0 to 26, as said below
- start: float32 [32, 8, 12, 64, 128], P('gx', 'gy', 'gz'), may hold values from -1800 to 1800
- velocity: float32 [32, 8, 12, 3, 16], P('gx', 'gy', 'gz'), may hold values from -6 to 6
- design: float32 [32, 8, 12, 16], P('gx', 'gy', 'gz'), may hold values from 0.05 to 1
- mask: int32 [32, 8, 12, 16], P('gx', 'gy', 'gz'), may hold values 0 or 1
Outputs:
- adjoint: float32 [32, 8, 12, 64, 128], P('gx', 'gy', 'gz')
- hessenberg: float32 [5, 128], replicated
- sensitivity: float32 [32, 8, 12, 16, 128], P('gx', 'gy', 'gz')
The draws below stay inside these ranges and needn't reach their ends.
Inputs may be any that keep to these rules, and one draw needn't show every extreme that they name: `columns`: the 27 slots of each block row name every offset code once.
All inputs are finite; a program needn't handle non-finite values. No bound on the sum of `mask` on one device may be relied on, other than what follows from the above.
Results may differ from the reference program's by a relative error of at most 0.0057.
Values sent between devices are 32-bit elements; how exact they have to be, the bound alone decides.
A program may use at most 64 MiB of HBM per device.

```python
import math
import jax
import jax.numpy as jnp
from jax import lax

RHS = 128
CELLS = 16
PATTERN = 27
BS = 64
NX = 32
NY = 8
NZ = 12


def slot_codes(key):
    code_key = jax.random.fold_in(key, 101)
    scores = jax.random.randint(code_key, (NX, NY, NZ, PATTERN), 0, 1048576, jnp.int32)
    scores = scores * 32 + jnp.arange(PATTERN, dtype=jnp.int32)
    return jnp.argsort(scores, axis=-1).astype(jnp.int32)


def draw_columns(key, part):
    codes = slot_codes(key)
    return codes


def draw_jacobian(key, part):
    codes = slot_codes(key)
    key = jax.random.fold_in(key, 7)
    identity_block = jnp.eye(BS, dtype=jnp.float32)
    noise_scale = 0.4 / math.sqrt(PATTERN * BS)

    def one_slab(index):
        slab_key = jax.random.fold_in(key, index)
        key_noise, key_diag = jax.random.split(slab_key)
        noise = jnp.clip(jax.random.normal(key_noise, (NY, NZ, BS, PATTERN, BS), jnp.float32), -6.0, 6.0)
        noise = jnp.clip(noise * noise_scale, -0.05, 0.05)
        diag_values = 0.1 * jnp.exp(jax.random.uniform(key_diag, (NY, NZ, BS), jnp.float32) * math.log(10.0))
        self_slot = (codes[index] == 13).astype(jnp.float32)
        added = diag_values[:, :, :, None, None] * self_slot[:, :, None, :, None] * identity_block[None, None, :, None, :]
        return (noise + added).reshape(NY, NZ, BS, PATTERN * BS).astype(jnp.bfloat16)
    return lax.map(one_slab, jnp.arange(NX, dtype=jnp.int32))


def draw_start(key, part):
    key = jax.random.fold_in(key, 3)
    key_base, key_block, key_column = jax.random.split(key, 3)
    block_scale = jnp.exp(jax.random.uniform(key_block, (NX, NY, NZ, 1, 1), jnp.float32) * math.log(10.0))
    column_scale = jnp.exp(jax.random.uniform(key_column, (1, 1, 1, 1, RHS), jnp.float32) * math.log(10.0))
    position = jnp.arange(NX, dtype=jnp.float32) / max(NX - 1, 1)
    ramp = jnp.exp(position * math.log(3.0)).reshape(NX, 1, 1, 1, 1)
    base = jax.random.normal(key_base, (NX, NY, NZ, BS, RHS), jnp.float32)
    base = jnp.clip(base, -6.0, 6.0)
    return (base * block_scale * column_scale * ramp).astype(jnp.float32)


def touch_ends(values, key, least, top_value):
    longest = values.shape.index(max(values.shape))
    spots = []
    for shift in (0, 1):
        where = [jax.random.randint(jax.random.fold_in(key, axis), (), 0, length) for axis, length in enumerate(values.shape)]
        where[longest] = (where[longest] + shift) % values.shape[longest]
        spots.append(tuple(where))
    return values.at[spots[0]].set(least).at[spots[1]].set(top_value)


def block_levels(rng, dims, cuts, low, high):
    gain, own = 1.0, jax.random.fold_in(rng, 6)
    for dim, blocks in cuts:
        heights = jnp.exp(jax.random.uniform(jax.random.fold_in(own, dim), (blocks,), jnp.float32, low / len(cuts), high / len(cuts)))
        gain = gain * jnp.repeat(heights, dims[dim] // blocks).reshape([-1 if axis == dim else 1 for axis in range(len(dims))])
    return gain


def bell_draw(rng, dims, scale, bound, cuts=(), held_as=jnp.bfloat16):
    drawn = jax.random.normal(rng, dims, jnp.float32) * scale
    if len(cuts) > 0:
        drawn = block_levels(rng, dims, cuts, -0.22, 0.18) * drawn
    return jnp.clip(drawn, min=-bound, max=bound).astype(held_as)


def setup_inputs(seed: int = 0) -> dict:
    splits = jax.random.split(jax.random.key(seed), 7)
    jacobian = draw_jacobian(jax.random.fold_in(splits[6], 71), 0)
    columns = draw_columns(jax.random.fold_in(splits[6], 71), 0)
    start = draw_start(jax.random.fold_in(splits[6], 71), 0)
    velocity = bell_draw(splits[3], (NX, NY, NZ, 3, CELLS), 1.0, 6.0, ((0, 32), (1, 2), (2, 4)), jnp.float32)
    design = jnp.clip(0.05 + 0.95 * jax.random.uniform(splits[4], (NX, NY, NZ, CELLS), jnp.float32) ** block_levels(splits[4], (NX, NY, NZ, CELLS), ((0, 32), (1, 2), (2, 4)), -0.2, 0.2), 0.05, 1.0)
    mask = touch_ends((jax.random.randint(splits[5], (NX, NY, NZ, CELLS), 0, 4) < 3).astype(jnp.int32), jax.random.fold_in(splits[5], 1), 0, 1)
    return dict(jacobian=jacobian, columns=columns, start=start, velocity=velocity, design=design, mask=mask)


epsilon = 1e-06

def transpose_apply(jacobian, columns, field):
    size_x, size_y, size_z = (field.shape[0], field.shape[1], field.shape[2])
    width = field.shape[3]
    count_rhs = field.shape[4]
    slots = columns.shape[3]
    blocks = jacobian.reshape(size_x, size_y, size_z, width, slots, width)
    field_low = lax.optimization_barrier(field.astype(jnp.bfloat16)).astype(jnp.float32)
    order_ids = jnp.arange(slots, dtype=jnp.int32)
    pushed = jnp.zeros((size_x + 2, size_y + 2, size_z + 2, width, count_rhs), jnp.float32)
    for offset in range(slots):
        step_x = offset // 9 - 1
        step_y = offset // 3 % 3 - 1
        step_z = offset % 3 - 1
        slot_index = lax.optimization_barrier(jnp.sum(jnp.where(columns == offset, order_ids, 0), axis=-1)).astype(jnp.int32)
        chosen = jnp.take_along_axis(blocks, slot_index[:, :, :, None, None, None], axis=4)[:, :, :, :, 0, :]
        product = jnp.einsum('abcij,abcir->abcjr', chosen.astype(jnp.float32), field_low)
        pushed = pushed.at[1 + step_x:1 + step_x + size_x, 1 + step_y:1 + step_y + size_y, 1 + step_z:1 + step_z + size_z].add(product)
    return pushed[1:-1, 1:-1, 1:-1]

def average(left, right):
    entries = left.shape[0] * left.shape[1] * left.shape[2] * left.shape[3]
    return lax.optimization_barrier(jnp.sum(left * right, axis=(0, 1, 2, 3))) / entries

def reference(jacobian, columns, start, velocity, design, mask):
    scale = jnp.sqrt(average(start, start) + epsilon)
    first = start / scale
    wide_one = transpose_apply(jacobian, columns, start) / scale
    coef_one = average(wide_one, first)
    rest_one = wide_one - coef_one * first
    norm_one = jnp.sqrt(average(rest_one, rest_one) + epsilon)
    second = rest_one / norm_one
    wide_two = transpose_apply(jacobian, columns, second)
    coef_two = average(wide_two, first)
    coef_three = average(wide_two, second)
    rest_two = wide_two - coef_two * first - coef_three * second
    norm_two = jnp.sqrt(average(rest_two, rest_two) + epsilon)
    adjoint = rest_two / norm_two
    hessenberg = jnp.stack([coef_one, norm_one, coef_two, coef_three, norm_two])
    cells = design.shape[3]
    shaped = adjoint.reshape(adjoint.shape[0], adjoint.shape[1], adjoint.shape[2], adjoint.shape[3] // cells, cells, adjoint.shape[4])
    dotted = lax.optimization_barrier(jnp.sum(velocity[..., None] * shaped[:, :, :, 0:3], axis=3))
    slope = -0.11 / ((0.1 + design) * (0.1 + design))
    sensitivity = (mask.astype(jnp.float32) * slope)[..., None] * dotted
    return (adjoint, hessenberg, sensitivity)
```

```python
import functools

import jax
import jax.numpy as jnp
from jax import lax
from jax.experimental import pallas as pl
from jax.experimental.pallas import tpu as pltpu
from jax.sharding import PartitionSpec as P

MESH = pl.DeviceIdType.MESH
epsilon = 1e-06
SLOTS = 27
WIDTH = 64
RHS = 128
ROWS_Y = 4
ROWS_Z = 3
TILE_SLOTS = 9
UP, DOWN = 0, 1


def divided(value, by):
    safe = by > 0
    return jnp.where(safe, value / jnp.where(safe, by, 1.0), 0.0)


def fitted(g11, g12, g22, a1, a2):
    det = g11 * g22 - g12 * g12
    good = det > 1e-4 * g11 * g22
    c2 = jnp.where(good, (g11 * a2 - g12 * a1) / jnp.where(good, det, 1.0), 0.0)
    return divided(a1 - g12 * c2, g11), c2


def total(value):
    return jnp.sum(value, axis=0)


def merged_one(g, c, r, e):
    whole = total(g)
    inner = total(g * c + e)
    centre = divided(inner, whole)
    d = c - centre
    return whole, centre, total(r + d * (2.0 * e + d * g)), total(e + d * g), inner


def merged_two(g11, g12, g22, c1, c2, r, e1, e2):
    w11, w12, w22 = total(g11), total(g12), total(g22)
    a1 = total(g11 * c1 + g12 * c2 + e1)
    a2 = total(g12 * c1 + g22 * c2 + e2)
    k1, k2 = fitted(w11, w12, w22, a1, a2)
    d1, d2 = c1 - k1, c2 - k2
    p1 = d1 * g11 + d2 * g12
    p2 = d1 * g12 + d2 * g22
    rest = total(r + d1 * (2.0 * e1 + p1) + d2 * (2.0 * e2 + p2))
    return w11, w12, w22, k1, k2, rest, total(e1 + p1), total(e2 + p2), a1, a2


def rows_of(block):
    return [block[:, k : k + 1, :] for k in range(8)]


def kernel(
    nx, ny, nz, low_count,
    inv_ref, j_ref, start_ref,
    rest_ref, hess_ref,
    jv, jt, prod, push, zrecv, xrecv, yrecv, field, second, plane_buf, line_buf,
    jsem, ssem, zs, zr, xs, xr, ys, yr, gs, gr,
):
    gx = lax.axis_index("gx")
    gy = lax.axis_index("gy")
    gz = lax.axis_index("gz")
    entries = float(nx * ny * nz * ROWS_Y * ROWS_Z * WIDTH)

    field_copy = pltpu.make_async_copy(start_ref, field, ssem)
    field_copy.start()

    def j_copy(order, cz):
        return pltpu.make_async_copy(j_ref.at[:, cz], jv.at[cz], jsem.at[order])

    cz_order = (0, 2, 1)
    for order, cz in enumerate(cz_order):
        j_copy(order, cz).start()

    high_count = nx // low_count
    n1 = nz * low_count
    n2 = ny * high_count
    gx_low = lax.rem(gx, low_count)
    gx_high = gx // low_count
    me1 = gz * low_count + gx_low
    me2 = gy * high_count + gx_high

    def peer1(step):
        p = lax.rem(me1 + step, n1)
        return (gx_high * low_count + lax.rem(p, low_count), gy, p // low_count)

    def peer2(step):
        p = lax.rem(me2 + step, n2)
        return (lax.rem(p, high_count) * low_count + gx_low, p // high_count, gz)

    barrier = pltpu.get_barrier_semaphore()

    def greet(device):
        pl.semaphore_signal(barrier, inc=1, device_id=device, device_id_type=MESH)

    for step in range(1, n1):
        greet(peer1(step))
    for step in range(1, n2):
        greet(peer2(step))

    below_outside = jnp.logical_and(gx > 0, gx_low == 0)
    above_outside = jnp.logical_and(gx < nx - 1, gx_low == low_count - 1)

    @pl.when(below_outside)
    def _():
        greet((gx - 1, gy, gz))

    @pl.when(above_outside)
    def _():
        greet((gx + 1, gy, gz))

    greeted = (
        n1 - 1 + n2 - 1 + jnp.where(below_outside, 1, 0) + jnp.where(above_outside, 1, 0)
    )

    def met():
        pl.semaphore_wait(barrier, greeted)

    has_z = (gz < nz - 1, gz > 0)
    from_z = (gz > 0, gz < nz - 1)
    halo_row = jnp.where(gy == 0, ROWS_Y - 1, 0)
    halo_step = jnp.where(gy == 0, 2, 0)

    def z_copy(t, way, dx):
        to = gz + 1 if way == UP else gz - 1
        return pltpu.make_async_remote_copy(
            src_ref=push.at[t, dx, 4 if way == UP else 0],
            dst_ref=zrecv.at[t, way, dx],
            send_sem=zs.at[t, way, dx],
            recv_sem=zr.at[t, way, dx],
            device_id=(gx, gy, to),
            device_id_type=MESH,
        )

    def x_copy(t, way, z):
        to = gx + 1 if way == UP else gx - 1
        return pltpu.make_async_remote_copy(
            src_ref=push.at[t, 2 if way == UP else 0, z],
            dst_ref=xrecv.at[t, way, z - 1],
            send_sem=xs.at[t, way, z - 1],
            recv_sem=xr.at[t, way, z - 1],
            device_id=(to, gy, gz),
            device_id_type=MESH,
        )

    has_x = (gx < nx - 1, gx > 0)
    from_x = (gx > 0, gx < nx - 1)

    def y_copy(t, z):
        return pltpu.make_async_remote_copy(
            src_ref=push.at[t, 1, z, ROWS_Y],
            dst_ref=yrecv.at[t, z - 1],
            send_sem=ys.at[t, z - 1],
            recv_sem=yr.at[t, z - 1],
            device_id=(gx, 1 - gy, gz),
            device_id_type=MESH,
        )

    def product(b, cz, offset):
        slot = inv_ref[b * ROWS_Z + cz, offset]
        return prod[cz, b, slot]

    def gather_plane(t, dx, z):
        for y in range(ROWS_Y + 1):
            value = None
            for cz in range(max(0, z - 2), min(ROWS_Z - 1, z) + 1):
                oz = z - cz
                if y == ROWS_Y:
                    pairs = [(halo_row, halo_step)]
                else:
                    pairs = [
                        (b, y + 1 - b) for b in range(max(0, y - 1), min(ROWS_Y - 1, y + 1) + 1)
                    ]
                for b, oy in pairs:
                    term = product(b, cz, dx * 9 + oy * 3 + oz)
                    value = term if value is None else value + term
            push[t, dx, z, y] = value

    def multiply(t, cz):
        source = field if t == 0 else second
        for half in range(ROWS_Y // 2):
            q = cz * 2 + half
            if t == 0:
                for column in range(0, SLOTS * WIDTH, 128):
                    size = min(128, SLOTS * WIDTH - column)
                    both = jnp.concatenate(
                        [
                            jv[cz, 2 * half, :, column : column + size],
                            jv[cz, 2 * half + 1, :, column : column + size],
                        ],
                        axis=0,
                    )
                    jt[q, column : column + size, :] = both.T
            one = source[2 * half, cz].astype(jnp.bfloat16)
            two = source[2 * half + 1, cz].astype(jnp.bfloat16)
            none = jnp.zeros_like(one)
            weights = jnp.concatenate(
                [jnp.concatenate([one, none], axis=1), jnp.concatenate([none, two], axis=1)], axis=0
            )
            for slot in range(0, SLOTS, TILE_SLOTS):
                out = jnp.dot(
                    jt[q, slot * WIDTH : (slot + TILE_SLOTS) * WIDTH, :],
                    weights,
                    preferred_element_type=jnp.float32,
                )
                tile = (TILE_SLOTS, WIDTH, RHS)
                prod[cz, 2 * half, slot : slot + TILE_SLOTS] = out[:, :RHS].reshape(tile)
                prod[cz, 2 * half + 1, slot : slot + TILE_SLOTS] = out[:, RHS:].reshape(tile)

    def start_if(condition, copy):
        @pl.when(condition)
        def _():
            copy.start()

    def apply(t):
        for order, cz in enumerate(cz_order):
            if t == 0:
                if order == 0:
                    field_copy.wait()
                j_copy(order, cz).wait()
            multiply(t, cz)
            if t == 0 and order == 0:
                met()
            if cz != 1:
                way, z = (DOWN, 0) if cz == 0 else (UP, 4)
                for dx in (0, 2):
                    gather_plane(t, dx, z)
                    start_if(has_z[way], z_copy(t, way, dx))
        for way, dx in ((UP, 2), (DOWN, 0)):
            gather_plane(t, dx, 2)
            start_if(has_x[way], x_copy(t, way, 2))
        for z in (3, 1):
            for way, dx in ((UP, 2), (DOWN, 0)):
                gather_plane(t, dx, z)
        for way, z in ((DOWN, 0), (UP, 4)):
            gather_plane(t, 1, z)
            start_if(has_z[way], z_copy(t, way, 1))
        for z in (2, 3, 1):
            gather_plane(t, 1, z)
        for way, z in ((DOWN, 3), (UP, 1)):
            for x_way, dx in ((DOWN, 0), (UP, 2)):

                @pl.when(from_z[way])
                def _():
                    z_copy(t, way, dx).wait_recv()
                    push[t, dx, z] = push[t, dx, z] + zrecv[t, way, dx]

                start_if(has_x[x_way], x_copy(t, x_way, z))
        for way, z in ((DOWN, 3), (UP, 1)):

            @pl.when(from_z[way])
            def _():
                z_copy(t, way, 1).wait_recv()
                push[t, 1, z] = push[t, 1, z] + zrecv[t, way, 1]

        for z in (2, 3, 1):
            for way in (UP, DOWN):

                @pl.when(from_x[way])
                def _():
                    x_copy(t, way, z).wait_recv()
                    push[t, 1, z] = push[t, 1, z] + xrecv[t, way, z - 1]

            y_copy(t, z).start()
        for z in (2, 3, 1):
            y_copy(t, z).wait_recv()
            push[t, 1, z, halo_row] = push[t, 1, z, halo_row] + yrecv[t, z - 1]

    def finish(t):
        for way in (UP, DOWN):

            @pl.when(has_z[way])
            def _():
                for dx in range(3):
                    z_copy(t, way, dx).wait_send()

            @pl.when(has_x[way])
            def _():
                for z in range(1, 4):
                    x_copy(t, way, z).wait_send()

        for z in range(1, 4):
            y_copy(t, z).wait_send()

    def wide(t, b, cz):
        return push[t, 1, cz + 1, b]

    cells = [(b, cz) for b in range(ROWS_Y) for cz in range(ROWS_Z)]

    def summed(terms):
        acc = None
        for term in terms:
            acc = term if acc is None else acc + term
        return jnp.sum(acc, axis=0, keepdims=True)

    def exchange(buf, t, stage, me, peer, count):
        def copy(step):
            return pltpu.make_async_remote_copy(
                src_ref=buf.at[t, me],
                dst_ref=buf.at[t, me],
                send_sem=gs.at[t, stage],
                recv_sem=gr.at[t, stage],
                device_id=peer(step),
                device_id_type=MESH,
            )

        for step in range(1, count):
            copy(step).start()
        every = pltpu.make_async_remote_copy(
            src_ref=buf.at[t, pl.ds(0, count - 1)],
            dst_ref=buf.at[t, pl.ds(0, count - 1)],
            send_sem=gs.at[t, stage],
            recv_sem=gr.at[t, stage],
            device_id=peer(1),
            device_id_type=MESH,
        )
        every.wait_send()
        every.wait_recv()
        return rows_of(buf[t])

    def put(buf, t, me, rows):
        blank = [jnp.zeros((1, RHS), jnp.float32)] * (8 - len(rows))
        buf[t, me] = jnp.concatenate(list(rows) + blank, axis=0)

    apply(0)
    g = summed(field[b, cz] * field[b, cz] for b, cz in cells)
    a = summed(wide(0, b, cz) * field[b, cz] for b, cz in cells)
    c = divided(a, g)
    r = summed((wide(0, b, cz) - c * field[b, cz]) ** 2 for b, cz in cells)
    e = summed((wide(0, b, cz) - c * field[b, cz]) * field[b, cz] for b, cz in cells)
    put(plane_buf, 0, me1, (g, c, r, e))
    rows = exchange(plane_buf, 0, 0, me1, peer1, n1)
    put(line_buf, 0, me2, merged_one(*rows[:4])[:4])
    rows = exchange(line_buf, 0, 1, me2, peer2, n2)
    g, c, r, e, a = merged_one(*rows[:4])
    scale_square = g / entries + epsilon
    scale = jnp.sqrt(scale_square)
    coef_one = a / entries / scale_square
    d = c - coef_one
    r = jnp.maximum(r + d * (2.0 * e + d * g), 0.0)
    norm_one = jnp.sqrt(r / entries / scale_square + epsilon)
    inv_scale = 1.0 / scale
    inv_second = 1.0 / norm_one
    for b, cz in cells:
        first = field[b, cz] * inv_scale
        second[b, cz] = (wide(0, b, cz) * inv_scale - coef_one * first) * inv_second
        field[b, cz] = first

    apply(1)
    g11 = summed(field[b, cz] * field[b, cz] for b, cz in cells)
    g12 = summed(field[b, cz] * second[b, cz] for b, cz in cells)
    g22 = summed(second[b, cz] * second[b, cz] for b, cz in cells)
    a1 = summed(wide(1, b, cz) * field[b, cz] for b, cz in cells)
    a2 = summed(wide(1, b, cz) * second[b, cz] for b, cz in cells)
    c1, c2 = fitted(g11, g12, g22, a1, a2)
    for b, cz in cells:
        rest_ref[b, cz] = wide(1, b, cz) - c1 * field[b, cz] - c2 * second[b, cz]
    r = summed(rest_ref[b, cz] * rest_ref[b, cz] for b, cz in cells)
    e1 = summed(rest_ref[b, cz] * field[b, cz] for b, cz in cells)
    e2 = summed(rest_ref[b, cz] * second[b, cz] for b, cz in cells)
    put(plane_buf, 1, me1, (g11, g12, g22, c1, c2, r, e1, e2))
    rows = exchange(plane_buf, 1, 0, me1, peer1, n1)
    put(line_buf, 1, me2, merged_two(*rows)[:8])
    rows = exchange(line_buf, 1, 1, me2, peer2, n2)
    g11, g12, g22, c1, c2, r, e1, e2, a1, a2 = merged_two(*rows)
    coef_two = a1 / entries
    coef_three = a2 / entries
    d1, d2 = c1 - coef_two, c2 - coef_three
    p1 = d1 * g11 + d2 * g12
    p2 = d1 * g12 + d2 * g22
    r = jnp.maximum(r + d1 * (2.0 * e1 + p1) + d2 * (2.0 * e2 + p2), 0.0)
    norm_two = jnp.sqrt(r / entries + epsilon)
    for b, cz in cells:
        rest_ref[b, cz] = wide(1, b, cz) - coef_two * field[b, cz] - coef_three * second[b, cz]
    hess_ref[...] = jnp.concatenate(
        [coef_one, norm_one, coef_two, coef_three, norm_two, norm_two, norm_two, norm_two], axis=0
    )
    finish(0)
    finish(1)


def per_device(nx, ny, nz, jacobian, columns, start, velocity, design, mask):
    low_count = min(4, nx)
    n1 = nz * low_count
    n2 = ny * (nx // low_count)
    flat = columns.reshape(ROWS_Y * ROWS_Z, SLOTS)
    order_ids = jnp.arange(SLOTS, dtype=jnp.int32)
    hits = flat[:, None, :] == order_ids[:, None]
    inverse = jnp.sum(jnp.where(hits, order_ids, 0), axis=-1)
    block = (WIDTH, RHS)
    f32 = jnp.float32
    rest, hess = pl.pallas_call(
        functools.partial(kernel, nx, ny, nz, low_count),
        out_shape=(
            jax.ShapeDtypeStruct((ROWS_Y, ROWS_Z) + block, f32),
            jax.ShapeDtypeStruct((8, RHS), f32),
        ),
        in_specs=[
            pl.BlockSpec(memory_space=pltpu.SMEM),
            pl.BlockSpec(memory_space=pl.ANY),
            pl.BlockSpec(memory_space=pl.ANY),
        ],
        out_specs=(
            pl.BlockSpec(memory_space=pltpu.VMEM),
            pl.BlockSpec(memory_space=pltpu.VMEM),
        ),
        scratch_shapes=[
            pltpu.VMEM((ROWS_Z, ROWS_Y, WIDTH, SLOTS * WIDTH), jnp.bfloat16),
            pltpu.VMEM((ROWS_Z * ROWS_Y // 2, SLOTS * WIDTH, 2 * WIDTH), jnp.bfloat16),
            pltpu.VMEM((ROWS_Z, ROWS_Y, SLOTS) + block, f32),
            pltpu.VMEM((2, 3, ROWS_Z + 2, ROWS_Y + 1) + block, f32),
            pltpu.VMEM((2, 2, 3, ROWS_Y + 1) + block, f32),
            pltpu.VMEM((2, 2, ROWS_Z, ROWS_Y + 1) + block, f32),
            pltpu.VMEM((2, ROWS_Z) + block, f32),
            pltpu.VMEM((ROWS_Y, ROWS_Z) + block, f32),
            pltpu.VMEM((ROWS_Y, ROWS_Z) + block, f32),
            pltpu.VMEM((2, n1, 8, RHS), f32),
            pltpu.VMEM((2, n2, 8, RHS), f32),
            pltpu.SemaphoreType.DMA((3,)),
            pltpu.SemaphoreType.DMA,
            pltpu.SemaphoreType.DMA((2, 2, 3)),
            pltpu.SemaphoreType.DMA((2, 2, 3)),
            pltpu.SemaphoreType.DMA((2, 2, 3)),
            pltpu.SemaphoreType.DMA((2, 2, 3)),
            pltpu.SemaphoreType.DMA((2, 3)),
            pltpu.SemaphoreType.DMA((2, 3)),
            pltpu.SemaphoreType.DMA((2, 2)),
            pltpu.SemaphoreType.DMA((2, 2)),
        ],
        compiler_params=pltpu.CompilerParams(
            collective_id=0, has_side_effects=True, vmem_limit_bytes=48 * 1024 * 1024
        ),
    )(
        inverse,
        jacobian.reshape(ROWS_Y, ROWS_Z, WIDTH, SLOTS * WIDTH),
        start.reshape((ROWS_Y, ROWS_Z) + block),
    )
    hessenberg = hess[:5]
    adjoint = (rest / hess[4]).reshape(start.shape)
    cells = design.shape[3]
    shaped = adjoint.reshape(adjoint.shape[:3] + (WIDTH // cells, cells, RHS))
    dotted = jnp.sum(velocity[..., None] * shaped[:, :, :, 0:3], axis=3)
    slope = -0.11 / ((0.1 + design) * (0.1 + design))
    sensitivity = (mask.astype(f32) * slope)[..., None] * dotted
    return (adjoint, hessenberg, sensitivity)


def solution(mesh):
    shape = mesh.shape
    in_specs = (
        P("gx", "gy", "gz", None, None),
        P("gx", "gy", "gz", None),
        P("gx", "gy", "gz", None, None),
        P("gx", "gy", "gz", None, None),
        P("gx", "gy", "gz", None),
        P("gx", "gy", "gz", None),
    )
    out_specs = (P("gx", "gy", "gz", None, None), P(), P("gx", "gy", "gz", None, None))
    return jax.shard_map(
        functools.partial(per_device, shape["gx"], shape["gy"], shape["gz"]),
        mesh=mesh,
        in_specs=in_specs,
        out_specs=out_specs,
        check_vma=False,
    )
```

```python
import functools

import jax
import jax.numpy as jnp
from jax import lax
from jax.experimental import pallas as pl
from jax.experimental.pallas import tpu as pltpu
from jax.sharding import PartitionSpec as P

MESH = pl.DeviceIdType.MESH
epsilon = 1e-06
SLOTS = 27
WIDTH = 64
RHS = 128
ROWS_Y = 4
ROWS_Z = 3
TILE_SLOTS = 9
UP, DOWN = 0, 1


def divided(value, by):
    safe = by > 0
    return jnp.where(safe, value / jnp.where(safe, by, 1.0), 0.0)


def fitted(g11, g12, g22, a1, a2):
    det = g11 * g22 - g12 * g12
    good = det > 1e-4 * g11 * g22
    c2 = jnp.where(good, (g11 * a2 - g12 * a1) / jnp.where(good, det, 1.0), 0.0)
    return divided(a1 - g12 * c2, g11), c2


def total(value):
    return jnp.sum(value, axis=0)


def merged_one(g, c, r, e):
    whole = total(g)
    inner = total(g * c + e)
    centre = divided(inner, whole)
    d = c - centre
    return whole, centre, total(r + d * (2.0 * e + d * g)), total(e + d * g), inner


def merged_two(g11, g12, g22, c1, c2, r, e1, e2):
    w11, w12, w22 = total(g11), total(g12), total(g22)
    a1 = total(g11 * c1 + g12 * c2 + e1)
    a2 = total(g12 * c1 + g22 * c2 + e2)
    k1, k2 = fitted(w11, w12, w22, a1, a2)
    d1, d2 = c1 - k1, c2 - k2
    p1 = d1 * g11 + d2 * g12
    p2 = d1 * g12 + d2 * g22
    rest = total(r + d1 * (2.0 * e1 + p1) + d2 * (2.0 * e2 + p2))
    return w11, w12, w22, k1, k2, rest, total(e1 + p1), total(e2 + p2), a1, a2


def rows_of(block):
    return [block[:, k : k + 1, :] for k in range(8)]


def kernel(
    nx, ny, nz,
    codes_ref, j_ref, start_ref,
    rest_ref, hess_ref,
    inv_vmem, inv_ref, jv, jt, prod, push, near_buf, z_buf, far_buf, corner_buf, y_buf, field, second, image, plane_buf, line_buf,
    isem, jsem, ssem, ns, nr, zs, zr, zos, zor, ms, mr, fs, fr, cs, cr, ys, yr, gs, gr,
):
    gx = lax.axis_index("gx")
    gy = lax.axis_index("gy")
    gz = lax.axis_index("gz")
    entries = float(nx * ny * nz * ROWS_Y * ROWS_Z * WIDTH)

    field_copy = pltpu.make_async_copy(start_ref, field, ssem)

    def j_copy(order, cz):
        return pltpu.make_async_copy(j_ref.at[:, cz], jv.at[cz], jsem.at[order])

    cz_order = (0, 2, 1)
    j_copy(0, 0).start()
    field_copy.start()
    j_copy(1, 2).start()
    j_copy(2, 1).start()

    layers = nx // 4
    layer = gx // 4
    low = lax.rem(gx // 2, 2)
    core = lax.rem(gx, 2)
    chip_y = gy * 2 + low
    chips_y = ny * 2

    def distance(step, size):
        return min(step, size - step)

    n1, me1 = chips_y * nz, chip_y * nz + gz
    n2, me2 = layers * 2, layer * 2 + core
    steps1 = sorted(
        ((dy, dz) for dy in range(chips_y) for dz in range(nz) if dy or dz),
        key=lambda o: (-distance(o[0], chips_y) - distance(o[1], nz), o),
    )
    steps2 = sorted(
        ((dl, dc) for dl in range(layers) for dc in range(2) if dl or dc),
        key=lambda o: (-distance(o[0], layers), o),
    )

    def peer1(step):
        y = lax.rem(chip_y + step[0], chips_y)
        return ((layer * 2 + lax.rem(y, 2)) * 2 + core, y // 2, lax.rem(gz + step[1], nz))

    def peer2(step):
        other = lax.rem(layer + step[0], layers)
        return ((other * 2 + low) * 2 + lax.rem(core + step[1], 2), gy, gz)

    far = core * 2
    near = 2 - far
    far_x = gx + far - 1
    has_far = jnp.logical_and(far_x >= 0, far_x < nx)
    far_device = (far_x, gy, gz)
    corner_device = (far_x, 1 - gy, gz)
    near_device = (gx + near - 1, gy, gz)
    side_device = (gx, 1 - gy, gz)
    has_z = (gz < nz - 1, gz > 0)
    from_z = (gz > 0, gz < nz - 1)
    halo_row = jnp.where(gy == 0, ROWS_Y - 1, 0)
    halo_step = jnp.where(gy == 0, 2, 0)

    barrier = pltpu.get_barrier_semaphore()

    def greet(device):
        pl.semaphore_signal(barrier, inc=1, device_id=device, device_id_type=MESH)

    for step in steps1:
        greet(peer1(step))
    for step in steps2:
        greet(peer2(step))

    @pl.when(has_far)
    def _():
        greet(far_device)
        greet(corner_device)

    greeted = n1 - 1 + n2 - 1 + jnp.where(has_far, 2, 0)

    codes = jnp.concatenate([codes_ref[cz] for cz in range(ROWS_Z)], axis=0)
    place = lax.broadcasted_iota(jnp.int32, codes.shape, 1)
    inverse = jnp.zeros_like(codes)
    for code in range(SLOTS):
        slot = jnp.max(jnp.where(codes == code, place, 0), axis=1, keepdims=True)
        inverse = jnp.where(place == code, slot, inverse)
    inv_vmem[...] = jnp.zeros_like(inv_vmem)
    inv_vmem[: ROWS_Y * ROWS_Z, :SLOTS] = inverse
    inv_copy = pltpu.make_async_copy(inv_vmem, inv_ref, isem)
    inv_copy.start()

    def send(source, target, send_sem, recv_sem, device):
        return pltpu.make_async_remote_copy(
            src_ref=source,
            dst_ref=target,
            send_sem=send_sem,
            recv_sem=recv_sem,
            device_id=device,
            device_id_type=MESH,
        )

    def near_copy(t, z):
        return send(push.at[t, near, z], near_buf.at[t, z], ns.at[t, z], nr.at[t, z], near_device)

    def z_device(way):
        return (gx, gy, gz + 1 if way == UP else gz - 1)

    def z_far_copy(t, way, y):
        return send(
            push.at[t, far, 4 if way == UP else 0, y],
            z_buf.at[t, way, 0, y],
            zs.at[t, way, y],
            zr.at[t, way, y],
            z_device(way),
        )

    def z_own_copy(t, way, part):
        rows = pl.ds(ROWS_Y, 1) if part == 0 else pl.ds(0, ROWS_Y)
        return send(
            push.at[t, 1, 4 if way == UP else 0, rows],
            z_buf.at[t, way, 1, rows],
            zos.at[t, way, part],
            zor.at[t, way, part],
            z_device(way),
        )

    def middle_copy(t):
        return send(
            push.at[t, far, 2, pl.ds(0, ROWS_Y)], far_buf.at[t, 1], ms.at[t], mr.at[t], far_device
        )

    def far_copy(t, z, y):
        return send(
            push.at[t, far, z, y],
            far_buf.at[t, z - 1, y],
            fs.at[t, z // 2, y],
            fr.at[t, z // 2, y],
            far_device,
        )

    def corner_copy(t):
        return send(
            push.at[t, far, pl.ds(1, ROWS_Z), ROWS_Y],
            corner_buf.at[t],
            cs.at[t],
            cr.at[t],
            corner_device,
        )

    def y_copy(t):
        return send(
            push.at[t, 1, pl.ds(1, ROWS_Z), ROWS_Y], y_buf.at[t], ys.at[t], yr.at[t], side_device
        )

    def gather_plane(t, dx, z):
        for y in range(ROWS_Y + 1):
            value = None
            for cz in range(max(0, z - 2), min(ROWS_Z - 1, z) + 1):
                oz = z - cz
                if y == ROWS_Y:
                    pairs = [(halo_row, halo_step)]
                else:
                    pairs = [
                        (b, y + 1 - b) for b in range(max(0, y - 1), min(ROWS_Y - 1, y + 1) + 1)
                    ]
                for b, oy in pairs:
                    term = prod[cz, b, inv_ref[cz * ROWS_Y + b, dx * 9 + oy * 3 + oz]]
                    value = term if value is None else value + term
            push[t, dx, z, y] = value

    def terms(value):
        high = value.astype(jnp.bfloat16)
        return high, (value - high.astype(jnp.float32)).astype(jnp.bfloat16)

    def multiply(t, cz):
        for half in range(ROWS_Y // 2):
            q = cz * 2 + half
            if t == 0:
                for column in range(0, SLOTS * WIDTH, 128):
                    size = min(128, SLOTS * WIDTH - column)
                    both = jnp.concatenate(
                        [
                            jv[cz, 2 * half, :, column : column + size],
                            jv[cz, 2 * half + 1, :, column : column + size],
                        ],
                        axis=0,
                    ).T
                    jt[q, column : column + size, :128] = both
                    jt[q, column : column + size, 128:] = both
            one = terms(source(t, 2 * half, cz))
            two = terms(source(t, 2 * half + 1, cz))
            none = jnp.zeros_like(one[0])
            weights = jnp.concatenate(
                [
                    jnp.concatenate(pair, axis=1)
                    for k in range(2)
                    for pair in ([one[k], none], [none, two[k]])
                ],
                axis=0,
            )
            for slot in range(0, SLOTS, TILE_SLOTS):
                out = jnp.dot(
                    jt[q, slot * WIDTH : (slot + TILE_SLOTS) * WIDTH, :],
                    weights,
                    preferred_element_type=jnp.float32,
                )
                tile = (TILE_SLOTS, WIDTH, RHS)
                prod[cz, 2 * half, slot : slot + TILE_SLOTS] = out[:, :RHS].reshape(tile)
                prod[cz, 2 * half + 1, slot : slot + TILE_SLOTS] = out[:, RHS:].reshape(tile)

    def wide(t, b, cz):
        return push[t, 1, cz + 1, b]

    def source(t, b, cz):
        return field[b, cz] if t == 0 else wide(0, b, cz)

    def apply(t, beside, later):
        waiting = []

        def out(action):
            if t == 0:
                waiting.append(action)
            else:
                action()

        def out_z_far(way):
            @pl.when(has_z[way])
            def _():
                for y in range(ROWS_Y + 1):
                    z_far_copy(t, way, y).start()

        def out_middle():
            @pl.when(has_far)
            def _():
                middle_copy(t).start()

        for order, cz in enumerate(cz_order):
            if t == 0:
                j_copy(order, cz).wait()
                if order == 0:
                    field_copy.wait()
            multiply(t, cz)
            if t == 0 and order == 0:
                inv_copy.wait()
            if cz == 1:
                continue
            way, z = (DOWN, 0) if cz == 0 else (UP, 4)
            gather_plane(t, far, z)
            out(functools.partial(out_z_far, way))

        gather_plane(t, far, 2)
        out(out_middle)
        for z in (0, 4, 2, 3, 1):
            gather_plane(t, near, z)
            out(near_copy(t, z).start)
        gather_plane(t, far, 3)
        gather_plane(t, far, 1)
        for z in (0, 4, 2, 3, 1):
            gather_plane(t, 1, z)
        if t == 0:
            pl.semaphore_wait(barrier, greeted)
        for action in waiting:
            action()
        for way, z in ((DOWN, 0), (UP, 4)):
            near_copy(t, z).wait_recv()
            push[t, 1, z] = push[t, 1, z] + near_buf[t, z]

            @pl.when(has_z[way])
            def _():
                z_own_copy(t, way, 0).start()
                z_own_copy(t, way, 1).start()

        for z in (2, 3, 1):
            near_copy(t, z).wait_recv()
            push[t, 1, z] = push[t, 1, z] + near_buf[t, z]

        beside()

        for y in range(ROWS_Y + 1):
            for way, z in ((DOWN, 3), (UP, 1)):

                @pl.when(from_z[way])
                def _():
                    z_far_copy(t, way, y).wait_recv()
                    push[t, far, z, y] = push[t, far, z, y] + z_buf[t, way, 0, y]

                if y < ROWS_Y:

                    @pl.when(has_far)
                    def _():
                        far_copy(t, z, y).start()

        @pl.when(has_far)
        def _():
            corner_copy(t).start()

        for part in (0, 1):
            rows = slice(ROWS_Y, ROWS_Y + 1) if part == 0 else slice(0, ROWS_Y)
            for way, z in ((DOWN, 3), (UP, 1)):

                @pl.when(from_z[way])
                def _():
                    z_own_copy(t, way, part).wait_recv()
                    push[t, 1, z, rows] = push[t, 1, z, rows] + z_buf[t, way, 1, rows]

            if part == 0:
                y_copy(t).start()

        later()

        @pl.when(has_far)
        def _():
            middle_copy(t).wait_recv()
            push[t, 1, 2, :ROWS_Y] = push[t, 1, 2, :ROWS_Y] + far_buf[t, 1]
            for y in range(ROWS_Y):
                for z in (3, 1):
                    far_copy(t, z, y).wait_recv()
                    push[t, 1, z, y] = push[t, 1, z, y] + far_buf[t, z - 1, y]

        y_copy(t).wait_recv()
        for z in range(ROWS_Z):
            push[t, 1, z + 1, halo_row] = push[t, 1, z + 1, halo_row] + y_buf[t, z]

        @pl.when(has_far)
        def _():
            corner_copy(t).wait_recv()
            for z in range(ROWS_Z):
                push[t, 1, z + 1, halo_row] = push[t, 1, z + 1, halo_row] + corner_buf[t, z]

    def finish(t):
        for way in (UP, DOWN):

            @pl.when(has_z[way])
            def _():
                for y in range(ROWS_Y + 1):
                    z_far_copy(t, way, y).wait_send()
                for part in (0, 1):
                    z_own_copy(t, way, part).wait_send()

        for z in range(ROWS_Z + 2):
            near_copy(t, z).wait_send()

        @pl.when(has_far)
        def _():
            middle_copy(t).wait_send()
            corner_copy(t).wait_send()
            for y in range(ROWS_Y):
                for z in (3, 1):
                    far_copy(t, z, y).wait_send()

        y_copy(t).wait_send()

    cells = [(b, cz) for b in range(ROWS_Y) for cz in range(ROWS_Z)]

    def summed(terms):
        acc = None
        for term in terms:
            acc = term if acc is None else acc + term
        return jnp.sum(acc, axis=0, keepdims=True)

    stages = ((plane_buf, me1, peer1, steps1), (line_buf, me2, peer2, steps2))

    def exchange_start(t, stage):
        buf, me, peer, steps = stages[stage]
        for step in steps:
            send(
                buf.at[t, me], buf.at[t, me], gs.at[t, stage], gr.at[t, stage], peer(step)
            ).start()

    def exchange_end(t, stage):
        buf, me, peer, steps = stages[stage]
        every = buf.at[t, pl.ds(0, len(steps))]
        copy = send(every, every, gs.at[t, stage], gr.at[t, stage], peer(steps[0]))
        copy.wait_send()
        copy.wait_recv()
        return rows_of(buf[t])

    def put(buf, t, me, rows):
        blank = [jnp.zeros((1, RHS), jnp.float32)] * (8 - len(rows))
        buf[t, me] = jnp.concatenate(list(rows) + blank, axis=0)

    def first_sums():
        g = summed(field[b, cz] * field[b, cz] for b, cz in cells)
        a = summed(wide(0, b, cz) * field[b, cz] for b, cz in cells)
        c = divided(a, g)
        r = summed((wide(0, b, cz) - c * field[b, cz]) ** 2 for b, cz in cells)
        e = summed((wide(0, b, cz) - c * field[b, cz]) * field[b, cz] for b, cz in cells)
        put(plane_buf, 0, me1, (g, c, r, e))
        exchange_start(0, 0)

    def first_layer():
        rows = exchange_end(0, 0)
        put(line_buf, 0, me2, merged_one(*rows[:4])[:4])
        exchange_start(0, 1)

    def nothing():
        pass

    apply(0, nothing, nothing)
    apply(1, first_sums, first_layer)
    g, c, r, e, a = merged_one(*exchange_end(0, 1)[:4])
    scale_square = g / entries + epsilon
    scale = jnp.sqrt(scale_square)
    coef_one = a / entries / scale_square
    d = c - coef_one
    r = jnp.maximum(r + d * (2.0 * e + d * g), 0.0)
    norm_one = jnp.sqrt(r / entries / scale_square + epsilon)
    inv_scale = 1.0 / scale
    inv_second = 1.0 / norm_one
    for b, cz in cells:
        first = field[b, cz] * inv_scale
        wide_one = wide(0, b, cz) * inv_scale
        field[b, cz] = first
        second[b, cz] = (wide_one - coef_one * first) * inv_second
        image[b, cz] = (wide(1, b, cz) * inv_scale - coef_one * wide_one) * inv_second

    g11 = summed(field[b, cz] * field[b, cz] for b, cz in cells)
    g12 = summed(field[b, cz] * second[b, cz] for b, cz in cells)
    g22 = summed(second[b, cz] * second[b, cz] for b, cz in cells)
    a1 = summed(image[b, cz] * field[b, cz] for b, cz in cells)
    a2 = summed(image[b, cz] * second[b, cz] for b, cz in cells)
    c1, c2 = fitted(g11, g12, g22, a1, a2)
    for b, cz in cells:
        rest_ref[b, cz] = image[b, cz] - c1 * field[b, cz] - c2 * second[b, cz]
    r = summed(rest_ref[b, cz] * rest_ref[b, cz] for b, cz in cells)
    e1 = summed(rest_ref[b, cz] * field[b, cz] for b, cz in cells)
    e2 = summed(rest_ref[b, cz] * second[b, cz] for b, cz in cells)
    put(plane_buf, 1, me1, (g11, g12, g22, c1, c2, r, e1, e2))
    exchange_start(1, 0)
    put(line_buf, 1, me2, merged_two(*exchange_end(1, 0))[:8])
    exchange_start(1, 1)
    finish(0)
    finish(1)
    g11, g12, g22, c1, c2, r, e1, e2, a1, a2 = merged_two(*exchange_end(1, 1))
    coef_two = a1 / entries
    coef_three = a2 / entries
    d1, d2 = c1 - coef_two, c2 - coef_three
    p1 = d1 * g11 + d2 * g12
    p2 = d1 * g12 + d2 * g22
    r = jnp.maximum(r + d1 * (2.0 * e1 + p1) + d2 * (2.0 * e2 + p2), 0.0)
    norm_two = jnp.sqrt(r / entries + epsilon)
    for b, cz in cells:
        rest_ref[b, cz] = image[b, cz] - coef_two * field[b, cz] - coef_three * second[b, cz]
    hess_ref[...] = jnp.concatenate(
        [coef_one, norm_one, coef_two, coef_three, norm_two, norm_two, norm_two, norm_two], axis=0
    )


def per_device(nx, ny, nz, jacobian, columns, start, velocity, design, mask):
    n1 = nz * ny * 2
    n2 = nx // 2
    codes = jnp.transpose(columns, (0, 2, 1, 3)).reshape(ROWS_Z, ROWS_Y, SLOTS)
    block = (WIDTH, RHS)
    f32 = jnp.float32
    rest, hess = pl.pallas_call(
        functools.partial(kernel, nx, ny, nz),
        out_shape=(
            jax.ShapeDtypeStruct((ROWS_Y, ROWS_Z) + block, f32),
            jax.ShapeDtypeStruct((8, RHS), f32),
        ),
        in_specs=[
            pl.BlockSpec(memory_space=pltpu.VMEM),
            pl.BlockSpec(memory_space=pltpu.HBM),
            pl.BlockSpec(memory_space=pltpu.HBM),
        ],
        out_specs=(
            pl.BlockSpec(memory_space=pltpu.VMEM),
            pl.BlockSpec(memory_space=pltpu.VMEM),
        ),
        scratch_shapes=[
            pltpu.VMEM((16, 128), jnp.int32),
            pltpu.SMEM((16, 128), jnp.int32),
            pltpu.VMEM((ROWS_Z, ROWS_Y, WIDTH, SLOTS * WIDTH), jnp.bfloat16),
            pltpu.VMEM((ROWS_Z * ROWS_Y // 2, SLOTS * WIDTH, 4 * WIDTH), jnp.bfloat16),
            pltpu.VMEM((ROWS_Z, ROWS_Y, SLOTS) + block, f32),
            pltpu.VMEM((2, 3, ROWS_Z + 2, ROWS_Y + 1) + block, f32),
            pltpu.VMEM((2, ROWS_Z + 2, ROWS_Y + 1) + block, f32),
            pltpu.VMEM((2, 2, 2, ROWS_Y + 1) + block, f32),
            pltpu.VMEM((2, ROWS_Z, ROWS_Y) + block, f32),
            pltpu.VMEM((2, ROWS_Z) + block, f32),
            pltpu.VMEM((2, ROWS_Z) + block, f32),
            pltpu.VMEM((ROWS_Y, ROWS_Z) + block, f32),
            pltpu.VMEM((ROWS_Y, ROWS_Z) + block, f32),
            pltpu.VMEM((ROWS_Y, ROWS_Z) + block, f32),
            pltpu.VMEM((2, n1, 8, RHS), f32),
            pltpu.VMEM((2, n2, 8, RHS), f32),
            pltpu.SemaphoreType.DMA,
            pltpu.SemaphoreType.DMA((3,)),
            pltpu.SemaphoreType.DMA,
            pltpu.SemaphoreType.DMA((2, ROWS_Z + 2)),
            pltpu.SemaphoreType.DMA((2, ROWS_Z + 2)),
            pltpu.SemaphoreType.DMA((2, 2, ROWS_Y + 1)),
            pltpu.SemaphoreType.DMA((2, 2, ROWS_Y + 1)),
            pltpu.SemaphoreType.DMA((2, 2, 2)),
            pltpu.SemaphoreType.DMA((2, 2, 2)),
            pltpu.SemaphoreType.DMA((2,)),
            pltpu.SemaphoreType.DMA((2,)),
            pltpu.SemaphoreType.DMA((2, 2, ROWS_Y)),
            pltpu.SemaphoreType.DMA((2, 2, ROWS_Y)),
            pltpu.SemaphoreType.DMA((2,)),
            pltpu.SemaphoreType.DMA((2,)),
            pltpu.SemaphoreType.DMA((2,)),
            pltpu.SemaphoreType.DMA((2,)),
            pltpu.SemaphoreType.DMA((2, 2)),
            pltpu.SemaphoreType.DMA((2, 2)),
        ],
        compiler_params=pltpu.CompilerParams(
            collective_id=0, has_side_effects=True, vmem_limit_bytes=52 * 1024 * 1024
        ),
    )(
        codes,
        jacobian.reshape(ROWS_Y, ROWS_Z, WIDTH, SLOTS * WIDTH),
        start.reshape((ROWS_Y, ROWS_Z) + block),
    )
    hessenberg = hess[:5]
    adjoint = (rest / hess[4]).reshape(start.shape)
    cells = design.shape[3]
    shaped = adjoint.reshape(adjoint.shape[:3] + (WIDTH // cells, cells, RHS))
    dotted = jnp.sum(velocity[..., None] * shaped[:, :, :, 0:3], axis=3)
    slope = -0.11 / ((0.1 + design) * (0.1 + design))
    sensitivity = (mask.astype(f32) * slope)[..., None] * dotted
    return (adjoint, hessenberg, sensitivity)


def solution(mesh):
    shape = mesh.shape
    in_specs = (
        P("gx", "gy", "gz", None, None),
        P("gx", "gy", "gz", None),
        P("gx", "gy", "gz", None, None),
        P("gx", "gy", "gz", None, None),
        P("gx", "gy", "gz", None),
        P("gx", "gy", "gz", None),
    )
    out_specs = (P("gx", "gy", "gz", None, None), P(), P("gx", "gy", "gz", None, None))
    return jax.shard_map(
        functools.partial(per_device, shape["gx"], shape["gy"], shape["gz"]),
        mesh=mesh,
        in_specs=in_specs,
        out_specs=out_specs,
        check_vma=False,
    )
```

```python
import functools

import jax
import jax.numpy as jnp
from jax import lax
from jax.experimental import pallas as pl
from jax.experimental.pallas import tpu as pltpu
from jax.sharding import PartitionSpec as P

MESH = pl.DeviceIdType.MESH
epsilon = 1e-06
SLOTS = 27
WIDTH = 64
RHS = 128
ROWS_Y = 4
ROWS_Z = 3
TILE_SLOTS = 9
UP, DOWN = 0, 1


def divided(value, by):
    safe = by > 0
    return jnp.where(safe, value / jnp.where(safe, by, 1.0), 0.0)


def fitted(g11, g12, g22, a1, a2):
    det = g11 * g22 - g12 * g12
    good = det > 1e-4 * g11 * g22
    c2 = jnp.where(good, (g11 * a2 - g12 * a1) / jnp.where(good, det, 1.0), 0.0)
    return divided(a1 - g12 * c2, g11), c2


def total(value):
    return jnp.sum(value, axis=0)


def merged_one(g, c, r, e):
    whole = total(g)
    inner = total(g * c + e)
    centre = divided(inner, whole)
    d = c - centre
    return whole, centre, total(r + d * (2.0 * e + d * g)), total(e + d * g), inner


def merged_two(g11, g12, g22, c1, c2, r, e1, e2):
    w11, w12, w22 = total(g11), total(g12), total(g22)
    a1 = total(g11 * c1 + g12 * c2 + e1)
    a2 = total(g12 * c1 + g22 * c2 + e2)
    k1, k2 = fitted(w11, w12, w22, a1, a2)
    d1, d2 = c1 - k1, c2 - k2
    p1 = d1 * g11 + d2 * g12
    p2 = d1 * g12 + d2 * g22
    rest = total(r + d1 * (2.0 * e1 + p1) + d2 * (2.0 * e2 + p2))
    return w11, w12, w22, k1, k2, rest, total(e1 + p1), total(e2 + p2), a1, a2


def rows_of(block):
    return [block[:, k : k + 1, :] for k in range(8)]


def kernel(
    nx, ny, nz,
    codes_ref, j_ref, start_ref,
    rest_ref, hess_ref,
    inv_vmem, inv_ref, jv, jt, prod, push, near_buf, z_buf, far_buf, corner_buf, y_buf, field, second, image, plane_buf, line_buf,
    isem, jsem, ssem, ns, nr, zs, zr, zos, zor, ms, mr, fs, fr, cs, cr, ys, yr, gs, gr,
):
    gx = lax.axis_index("gx")
    gy = lax.axis_index("gy")
    gz = lax.axis_index("gz")
    entries = float(nx * ny * nz * ROWS_Y * ROWS_Z * WIDTH)

    layers = nx // 4
    layer = gx // 4
    low = lax.rem(gx // 2, 2)
    core = lax.rem(gx, 2)
    chip_y = gy * 2 + low
    chips_y = ny * 2

    def distance(step, size):
        return min(step, size - step)

    n1, me1 = chips_y * nz, chip_y * nz + gz
    n2, me2 = layers * 2, layer * 2 + core
    steps1 = sorted(
        ((dy, dz) for dy in range(chips_y) for dz in range(nz) if dy or dz),
        key=lambda o: (-distance(o[0], chips_y) - distance(o[1], nz), o),
    )
    steps2 = sorted(
        ((dl, dc) for dl in range(layers) for dc in range(2) if dl or dc),
        key=lambda o: (-distance(o[0], layers), o),
    )

    def peer1(step):
        y = lax.rem(chip_y + step[0], chips_y)
        return ((layer * 2 + lax.rem(y, 2)) * 2 + core, y // 2, lax.rem(gz + step[1], nz))

    def peer2(step):
        other = lax.rem(layer + step[0], layers)
        return ((other * 2 + low) * 2 + lax.rem(core + step[1], 2), gy, gz)

    far = core * 2
    near = 2 - far
    far_x = gx + far - 1
    has_far = jnp.logical_and(far_x >= 0, far_x < nx)
    far_device = (far_x, gy, gz)
    corner_device = (far_x, 1 - gy, gz)
    near_device = (gx + near - 1, gy, gz)
    side_device = (gx, 1 - gy, gz)
    has_z = (gz < nz - 1, gz > 0)
    from_z = (gz > 0, gz < nz - 1)
    halo_row = jnp.where(gy == 0, ROWS_Y - 1, 0)
    halo_step = jnp.where(gy == 0, 2, 0)

    barrier = pltpu.get_barrier_semaphore()

    def greet(device):
        pl.semaphore_signal(barrier, inc=1, device_id=device, device_id_type=MESH)

    for k in range(max(len(steps1), len(steps2))):
        if k < len(steps1):
            greet(peer1(steps1[k]))
        if k < len(steps2):
            greet(peer2(steps2[k]))

    @pl.when(has_far)
    def _():
        greet(far_device)
        greet(corner_device)

    greeted = n1 - 1 + n2 - 1 + jnp.where(has_far, 2, 0)

    field_copy = pltpu.make_async_copy(start_ref, field, ssem)

    def j_copy(order, cz):
        return pltpu.make_async_copy(j_ref.at[:, cz], jv.at[cz], jsem.at[order])

    cz_order = (0, 2, 1)
    j_copy(0, 0).start()
    field_copy.start()
    j_copy(1, 2).start()
    j_copy(2, 1).start()

    codes = jnp.concatenate([codes_ref[cz] for cz in range(ROWS_Z)], axis=0)
    place = lax.broadcasted_iota(jnp.int32, codes.shape, 1)
    inverse = jnp.zeros_like(codes)
    for code in range(SLOTS):
        slot = jnp.max(jnp.where(codes == code, place, 0), axis=1, keepdims=True)
        inverse = jnp.where(place == code, slot, inverse)
    inv_vmem[...] = jnp.zeros_like(inv_vmem)
    inv_vmem[: ROWS_Y * ROWS_Z, :SLOTS] = inverse
    inv_copy = pltpu.make_async_copy(inv_vmem, inv_ref, isem)
    inv_copy.start()

    def send(source, target, send_sem, recv_sem, device):
        return pltpu.make_async_remote_copy(
            src_ref=source,
            dst_ref=target,
            send_sem=send_sem,
            recv_sem=recv_sem,
            device_id=device,
            device_id_type=MESH,
        )

    def near_copy(t, z):
        return send(push.at[t, near, z], near_buf.at[t, z], ns.at[t, z], nr.at[t, z], near_device)

    def z_device(way):
        return (gx, gy, gz + 1 if way == UP else gz - 1)

    def z_far_copy(t, way, y):
        return send(
            push.at[t, far, 4 if way == UP else 0, y],
            z_buf.at[t, way, 0, y],
            zs.at[t, way, y],
            zr.at[t, way, y],
            z_device(way),
        )

    def z_own_copy(t, way, part):
        rows = pl.ds(ROWS_Y, 1) if part == 0 else pl.ds(0, ROWS_Y)
        return send(
            push.at[t, 1, 4 if way == UP else 0, rows],
            z_buf.at[t, way, 1, rows],
            zos.at[t, way, part],
            zor.at[t, way, part],
            z_device(way),
        )

    def middle_copy(t):
        return send(
            push.at[t, far, 2, pl.ds(0, ROWS_Y)], far_buf.at[t, 1], ms.at[t], mr.at[t], far_device
        )

    def far_copy(t, z, y):
        return send(
            push.at[t, far, z, y],
            far_buf.at[t, z - 1, y],
            fs.at[t, z // 2, y],
            fr.at[t, z // 2, y],
            far_device,
        )

    def corner_copy(t):
        return send(
            push.at[t, far, pl.ds(1, ROWS_Z), ROWS_Y],
            corner_buf.at[t],
            cs.at[t],
            cr.at[t],
            corner_device,
        )

    def y_copy(t):
        return send(
            push.at[t, 1, pl.ds(1, ROWS_Z), ROWS_Y], y_buf.at[t], ys.at[t], yr.at[t], side_device
        )

    def gather_plane(t, dx, z):
        for y in range(ROWS_Y + 1):
            value = None
            for cz in range(max(0, z - 2), min(ROWS_Z - 1, z) + 1):
                oz = z - cz
                if y == ROWS_Y:
                    pairs = [(halo_row, halo_step)]
                else:
                    pairs = [
                        (b, y + 1 - b) for b in range(max(0, y - 1), min(ROWS_Y - 1, y + 1) + 1)
                    ]
                for b, oy in pairs:
                    term = prod[cz, b, inv_ref[cz * ROWS_Y + b, dx * 9 + oy * 3 + oz]]
                    value = term if value is None else value + term
            push[t, dx, z, y] = value

    def terms(value):
        high = value.astype(jnp.bfloat16)
        return high, (value - high.astype(jnp.float32)).astype(jnp.bfloat16)

    def multiply(t, cz):
        for half in range(ROWS_Y // 2):
            q = cz * 2 + half
            if t == 0:
                for column in range(0, SLOTS * WIDTH, 128):
                    size = min(128, SLOTS * WIDTH - column)
                    both = jnp.concatenate(
                        [
                            jv[cz, 2 * half, :, column : column + size],
                            jv[cz, 2 * half + 1, :, column : column + size],
                        ],
                        axis=0,
                    ).T
                    jt[q, column : column + size, :128] = both
                    jt[q, column : column + size, 128:] = both
            one = terms(source(t, 2 * half, cz))
            two = terms(source(t, 2 * half + 1, cz))
            none = jnp.zeros_like(one[0])
            weights = jnp.concatenate(
                [
                    jnp.concatenate(pair, axis=1)
                    for k in range(2)
                    for pair in ([one[k], none], [none, two[k]])
                ],
                axis=0,
            )
            for slot in range(0, SLOTS, TILE_SLOTS):
                out = jnp.dot(
                    jt[q, slot * WIDTH : (slot + TILE_SLOTS) * WIDTH, :],
                    weights,
                    preferred_element_type=jnp.float32,
                )
                tile = (TILE_SLOTS, WIDTH, RHS)
                prod[cz, 2 * half, slot : slot + TILE_SLOTS] = out[:, :RHS].reshape(tile)
                prod[cz, 2 * half + 1, slot : slot + TILE_SLOTS] = out[:, RHS:].reshape(tile)

    def wide(t, b, cz):
        return push[t, 1, cz + 1, b]

    def source(t, b, cz):
        return field[b, cz] if t == 0 else wide(0, b, cz)

    def apply(t, beside, later, last):
        waiting = []

        def out(action):
            if t == 0:
                waiting.append(action)
            else:
                action()

        def out_z_far(way, rows=(0, ROWS_Y, 1)):
            @pl.when(has_z[way])
            def _():
                for y in rows:
                    z_far_copy(t, way, y).start()

        def out_middle():
            @pl.when(has_far)
            def _():
                middle_copy(t).start()

        for order, cz in enumerate(cz_order):
            if t == 0:
                j_copy(order, cz).wait()
                if order == 0:
                    field_copy.wait()
            multiply(t, cz)
            if t == 0 and order == 0:
                inv_copy.wait()
            if cz == 1:
                continue
            way, z = (DOWN, 0) if cz == 0 else (UP, 4)
            gather_plane(t, far, z)
            out(functools.partial(out_z_far, way))

        gather_plane(t, far, 2)
        out(out_middle)
        for z in (0, 4, 2, 3, 1):
            gather_plane(t, near, z)
            out(near_copy(t, z).start)
        gather_plane(t, far, 3)
        gather_plane(t, far, 1)
        for z in (0, 4, 2, 3, 1):
            gather_plane(t, 1, z)
        if t == 0:
            pl.semaphore_wait(barrier, greeted)
        for action in waiting:
            action()
        beside()
        for way, z in ((DOWN, 0), (UP, 4)):
            near_copy(t, z).wait_recv()
            push[t, 1, z] = push[t, 1, z] + near_buf[t, z]

            @pl.when(has_z[way])
            def _():
                z_own_copy(t, way, 0).start()

        for way in (DOWN, UP):
            out_z_far(way, (2, 3))

            @pl.when(has_z[way])
            def _():
                z_own_copy(t, way, 1).start()

        for z in (2, 3, 1):
            near_copy(t, z).wait_recv()
            push[t, 1, z] = push[t, 1, z] + near_buf[t, z]

        def from_z_far(y):
            for way, z in ((DOWN, 3), (UP, 1)):

                @pl.when(from_z[way])
                def _():
                    z_far_copy(t, way, y).wait_recv()
                    push[t, far, z, y] = push[t, far, z, y] + z_buf[t, way, 0, y]

                if y < ROWS_Y:

                    @pl.when(has_far)
                    def _():
                        far_copy(t, z, y).start()

        def from_z_own(part):
            rows = slice(ROWS_Y, ROWS_Y + 1) if part == 0 else slice(0, ROWS_Y)
            for way, z in ((DOWN, 3), (UP, 1)):

                @pl.when(from_z[way])
                def _():
                    z_own_copy(t, way, part).wait_recv()
                    push[t, 1, z, rows] = push[t, 1, z, rows] + z_buf[t, way, 1, rows]

        def from_far(y):
            @pl.when(has_far)
            def _():
                for z in (3, 1):
                    far_copy(t, z, y).wait_recv()
                    push[t, 1, z, y] = push[t, 1, z, y] + far_buf[t, z - 1, y]

        from_z_far(0)
        from_z_far(ROWS_Y)

        @pl.when(has_far)
        def _():
            corner_copy(t).start()

        from_z_far(1)
        from_z_own(0)
        y_copy(t).start()
        from_z_far(2)
        from_z_far(3)
        later()
        from_z_own(1)

        @pl.when(has_far)
        def _():
            middle_copy(t).wait_recv()
            push[t, 1, 2, :ROWS_Y] = push[t, 1, 2, :ROWS_Y] + far_buf[t, 1]

        from_far(0)

        @pl.when(has_far)
        def _():
            corner_copy(t).wait_recv()
            for z in range(ROWS_Z):
                push[t, 1, z + 1, halo_row] = push[t, 1, z + 1, halo_row] + corner_buf[t, z]

        from_far(1)
        y_copy(t).wait_recv()
        for z in range(ROWS_Z):
            push[t, 1, z + 1, halo_row] = push[t, 1, z + 1, halo_row] + y_buf[t, z]
        from_far(2)
        last()
        from_far(3)

    def finish(t):
        for way in (UP, DOWN):

            @pl.when(has_z[way])
            def _():
                for y in range(ROWS_Y + 1):
                    z_far_copy(t, way, y).wait_send()
                for part in (0, 1):
                    z_own_copy(t, way, part).wait_send()

        for z in range(ROWS_Z + 2):
            near_copy(t, z).wait_send()

        @pl.when(has_far)
        def _():
            middle_copy(t).wait_send()
            corner_copy(t).wait_send()
            for y in range(ROWS_Y):
                for z in (3, 1):
                    far_copy(t, z, y).wait_send()

        y_copy(t).wait_send()

    cells = [(b, cz) for b in range(ROWS_Y) for cz in range(ROWS_Z)]

    def summed(terms):
        acc = None
        for term in terms:
            acc = term if acc is None else acc + term
        return jnp.sum(acc, axis=0, keepdims=True)

    stages = ((plane_buf, me1, peer1, steps1), (line_buf, me2, peer2, steps2))

    def exchange_start(t, stage):
        buf, me, peer, steps = stages[stage]
        for step in steps:
            send(
                buf.at[t, me], buf.at[t, me], gs.at[t, stage], gr.at[t, stage], peer(step)
            ).start()

    def exchange_end(t, stage):
        buf, me, peer, steps = stages[stage]
        every = buf.at[t, pl.ds(0, len(steps))]
        copy = send(every, every, gs.at[t, stage], gr.at[t, stage], peer(steps[0]))
        copy.wait_send()
        copy.wait_recv()
        return rows_of(buf[t])

    def put(buf, t, me, rows):
        blank = [jnp.zeros((1, RHS), jnp.float32)] * (8 - len(rows))
        buf[t, me] = jnp.concatenate(list(rows) + blank, axis=0)

    def first_sums():
        g = summed(field[b, cz] * field[b, cz] for b, cz in cells)
        a = summed(wide(0, b, cz) * field[b, cz] for b, cz in cells)
        c = divided(a, g)
        r = summed((wide(0, b, cz) - c * field[b, cz]) ** 2 for b, cz in cells)
        e = summed((wide(0, b, cz) - c * field[b, cz]) * field[b, cz] for b, cz in cells)
        put(plane_buf, 0, me1, (g, c, r, e))
        exchange_start(0, 0)

    def first_layer():
        rows = exchange_end(0, 0)
        put(line_buf, 0, me2, merged_one(*rows[:4])[:4])
        exchange_start(0, 1)

    def nothing():
        pass

    found = []

    def first_end():
        g, c, r, e, a = merged_one(*exchange_end(0, 1)[:4])
        scale_square = g / entries + epsilon
        coef_one = a / entries / scale_square
        d = c - coef_one
        r = jnp.maximum(r + d * (2.0 * e + d * g), 0.0)
        norm_one = jnp.sqrt(r / entries / scale_square + epsilon)
        inv_scale = 1.0 / jnp.sqrt(scale_square)
        inv_second = 1.0 / norm_one
        for b, cz in cells:
            first = field[b, cz] * inv_scale
            wide_one = wide(0, b, cz) * inv_scale
            field[b, cz] = first
            second[b, cz] = (wide_one - coef_one * first) * inv_second
        g11 = summed(field[b, cz] * field[b, cz] for b, cz in cells)
        g12 = summed(field[b, cz] * second[b, cz] for b, cz in cells)
        g22 = summed(second[b, cz] * second[b, cz] for b, cz in cells)
        found.extend(
            (coef_one, norm_one, inv_scale * inv_second, coef_one * inv_scale * inv_second)
        )
        found.extend((g11, g12, g22))

    apply(0, nothing, nothing, nothing)
    apply(1, first_sums, first_layer, first_end)
    coef_one, norm_one, gain, shift, g11, g12, g22 = found

    for b, cz in cells:
        image[b, cz] = wide(1, b, cz) * gain - wide(0, b, cz) * shift
    a1 = summed(image[b, cz] * field[b, cz] for b, cz in cells)
    a2 = summed(image[b, cz] * second[b, cz] for b, cz in cells)
    c1, c2 = fitted(g11, g12, g22, a1, a2)
    for b, cz in cells:
        rest_ref[b, cz] = image[b, cz] - c1 * field[b, cz] - c2 * second[b, cz]
    r = summed(rest_ref[b, cz] * rest_ref[b, cz] for b, cz in cells)
    e1 = summed(rest_ref[b, cz] * field[b, cz] for b, cz in cells)
    e2 = summed(rest_ref[b, cz] * second[b, cz] for b, cz in cells)
    put(plane_buf, 1, me1, (g11, g12, g22, c1, c2, r, e1, e2))
    exchange_start(1, 0)
    put(line_buf, 1, me2, merged_two(*exchange_end(1, 0))[:8])
    exchange_start(1, 1)
    finish(0)
    finish(1)
    g11, g12, g22, c1, c2, r, e1, e2, a1, a2 = merged_two(*exchange_end(1, 1))
    coef_two = a1 / entries
    coef_three = a2 / entries
    d1, d2 = c1 - coef_two, c2 - coef_three
    p1 = d1 * g11 + d2 * g12
    p2 = d1 * g12 + d2 * g22
    r = jnp.maximum(r + d1 * (2.0 * e1 + p1) + d2 * (2.0 * e2 + p2), 0.0)
    norm_two = jnp.sqrt(r / entries + epsilon)
    for b, cz in cells:
        rest_ref[b, cz] = image[b, cz] - coef_two * field[b, cz] - coef_three * second[b, cz]
    hess_ref[...] = jnp.concatenate(
        [coef_one, norm_one, coef_two, coef_three, norm_two, norm_two, norm_two, norm_two], axis=0
    )


def per_device(nx, ny, nz, jacobian, columns, start, velocity, design, mask):
    n1 = nz * ny * 2
    n2 = nx // 2
    codes = jnp.transpose(columns, (0, 2, 1, 3)).reshape(ROWS_Z, ROWS_Y, SLOTS)
    block = (WIDTH, RHS)
    f32 = jnp.float32
    rest, hess = pl.pallas_call(
        functools.partial(kernel, nx, ny, nz),
        out_shape=(
            jax.ShapeDtypeStruct((ROWS_Y, ROWS_Z) + block, f32),
            jax.ShapeDtypeStruct((8, RHS), f32),
        ),
        in_specs=[
            pl.BlockSpec(memory_space=pltpu.VMEM),
            pl.BlockSpec(memory_space=pltpu.HBM),
            pl.BlockSpec(memory_space=pltpu.HBM),
        ],
        out_specs=(
            pl.BlockSpec(memory_space=pltpu.VMEM),
            pl.BlockSpec(memory_space=pltpu.VMEM),
        ),
        scratch_shapes=[
            pltpu.VMEM((16, 128), jnp.int32),
            pltpu.SMEM((16, 128), jnp.int32),
            pltpu.VMEM((ROWS_Z, ROWS_Y, WIDTH, SLOTS * WIDTH), jnp.bfloat16),
            pltpu.VMEM((ROWS_Z * ROWS_Y // 2, SLOTS * WIDTH, 4 * WIDTH), jnp.bfloat16),
            pltpu.VMEM((ROWS_Z, ROWS_Y, SLOTS) + block, f32),
            pltpu.VMEM((2, 3, ROWS_Z + 2, ROWS_Y + 1) + block, f32),
            pltpu.VMEM((2, ROWS_Z + 2, ROWS_Y + 1) + block, f32),
            pltpu.VMEM((2, 2, 2, ROWS_Y + 1) + block, f32),
            pltpu.VMEM((2, ROWS_Z, ROWS_Y) + block, f32),
            pltpu.VMEM((2, ROWS_Z) + block, f32),
            pltpu.VMEM((2, ROWS_Z) + block, f32),
            pltpu.VMEM((ROWS_Y, ROWS_Z) + block, f32),
            pltpu.VMEM((ROWS_Y, ROWS_Z) + block, f32),
            pltpu.VMEM((ROWS_Y, ROWS_Z) + block, f32),
            pltpu.VMEM((2, n1, 8, RHS), f32),
            pltpu.VMEM((2, n2, 8, RHS), f32),
            pltpu.SemaphoreType.DMA,
            pltpu.SemaphoreType.DMA((3,)),
            pltpu.SemaphoreType.DMA,
            pltpu.SemaphoreType.DMA((2, ROWS_Z + 2)),
            pltpu.SemaphoreType.DMA((2, ROWS_Z + 2)),
            pltpu.SemaphoreType.DMA((2, 2, ROWS_Y + 1)),
            pltpu.SemaphoreType.DMA((2, 2, ROWS_Y + 1)),
            pltpu.SemaphoreType.DMA((2, 2, 2)),
            pltpu.SemaphoreType.DMA((2, 2, 2)),
            pltpu.SemaphoreType.DMA((2,)),
            pltpu.SemaphoreType.DMA((2,)),
            pltpu.SemaphoreType.DMA((2, 2, ROWS_Y)),
            pltpu.SemaphoreType.DMA((2, 2, ROWS_Y)),
            pltpu.SemaphoreType.DMA((2,)),
            pltpu.SemaphoreType.DMA((2,)),
            pltpu.SemaphoreType.DMA((2,)),
            pltpu.SemaphoreType.DMA((2,)),
            pltpu.SemaphoreType.DMA((2, 2)),
            pltpu.SemaphoreType.DMA((2, 2)),
        ],
        compiler_params=pltpu.CompilerParams(
            collective_id=0, has_side_effects=True, vmem_limit_bytes=52 * 1024 * 1024
        ),
    )(
        codes,
        jacobian.reshape(ROWS_Y, ROWS_Z, WIDTH, SLOTS * WIDTH),
        start.reshape((ROWS_Y, ROWS_Z) + block),
    )
    hessenberg = hess[:5]
    adjoint = (rest / hess[4]).reshape(start.shape)
    cells = design.shape[3]
    shaped = adjoint.reshape(adjoint.shape[:3] + (WIDTH // cells, cells, RHS))
    dotted = jnp.sum(velocity[..., None] * shaped[:, :, :, 0:3], axis=3)
    slope = -0.11 / ((0.1 + design) * (0.1 + design))
    sensitivity = (mask.astype(f32) * slope)[..., None] * dotted
    return (adjoint, hessenberg, sensitivity)


def solution(mesh):
    shape = mesh.shape
    in_specs = (
        P("gx", "gy", "gz", None, None),
        P("gx", "gy", "gz", None),
        P("gx", "gy", "gz", None, None),
        P("gx", "gy", "gz", None, None),
        P("gx", "gy", "gz", None),
        P("gx", "gy", "gz", None),
    )
    out_specs = (P("gx", "gy", "gz", None, None), P(), P("gx", "gy", "gz", None, None))
    return jax.shard_map(
        functools.partial(per_device, shape["gx"], shape["gy"], shape["gz"]),
        mesh=mesh,
        in_specs=in_specs,
        out_specs=out_specs,
        check_vma=False,
    )
```

```python
import functools

import jax
import jax.numpy as jnp
from jax import lax
from jax.experimental import pallas as pl
from jax.experimental.pallas import tpu as pltpu
from jax.sharding import PartitionSpec as P

MESH = pl.DeviceIdType.MESH
epsilon = 1e-06
SLOTS = 27
WIDTH = 64
RHS = 128
ROWS_Y = 4
ROWS_Z = 3
TILE_SLOTS = 9
UP, DOWN = 0, 1


def divided(value, by):
    safe = by > 0
    return jnp.where(safe, value / jnp.where(safe, by, 1.0), 0.0)


def fitted(g11, g12, g22, a1, a2):
    det = g11 * g22 - g12 * g12
    good = det > 1e-4 * g11 * g22
    c2 = jnp.where(good, (g11 * a2 - g12 * a1) / jnp.where(good, det, 1.0), 0.0)
    return divided(a1 - g12 * c2, g11), c2


def total(value):
    return jnp.sum(value, axis=0)


def merged_one(g, c, r, e):
    whole = total(g)
    inner = total(g * c + e)
    centre = divided(inner, whole)
    d = c - centre
    return whole, centre, total(r + d * (2.0 * e + d * g)), total(e + d * g), inner


def merged_two(g11, g12, g22, c1, c2, r, e1, e2):
    w11, w12, w22 = total(g11), total(g12), total(g22)
    a1 = total(g11 * c1 + g12 * c2 + e1)
    a2 = total(g12 * c1 + g22 * c2 + e2)
    k1, k2 = fitted(w11, w12, w22, a1, a2)
    d1, d2 = c1 - k1, c2 - k2
    p1 = d1 * g11 + d2 * g12
    p2 = d1 * g12 + d2 * g22
    rest = total(r + d1 * (2.0 * e1 + p1) + d2 * (2.0 * e2 + p2))
    return w11, w12, w22, k1, k2, rest, total(e1 + p1), total(e2 + p2), a1, a2


def rows_of(block):
    return [block[:, k : k + 1, :] for k in range(8)]


def kernel(
    nx, ny, nz,
    codes_hbm, j_ref, start_ref,
    rest_ref, hess_ref,
    codes_ref, inv_vmem, inv_ref, jv, jt, prod, push, near_buf, z_buf, far_buf, corner_buf, y_buf, field, second, image, plane_buf, line_buf,
    csem, isem, jsem, ssem, ns, nr, zs, zr, zos, zor, ms, mr, fs, fr, cs, cr, ys, yr, gs, gr,
):
    gx = lax.axis_index("gx")
    gy = lax.axis_index("gy")
    gz = lax.axis_index("gz")
    entries = float(nx * ny * nz * ROWS_Y * ROWS_Z * WIDTH)

    layers = nx // 4
    layer = gx // 4
    low = lax.rem(gx // 2, 2)
    core = lax.rem(gx, 2)
    chip_y = gy * 2 + low
    chips_y = ny * 2

    def distance(step, size):
        return min(step, size - step)

    n1, me1 = chips_y * nz, chip_y * nz + gz
    n2, me2 = layers * 2, layer * 2 + core
    steps1 = sorted(
        ((dy, dz) for dy in range(chips_y) for dz in range(nz) if dy or dz),
        key=lambda o: (-distance(o[0], chips_y) - distance(o[1], nz), o),
    )
    steps2 = sorted(
        ((dl, dc) for dl in range(layers) for dc in range(2) if dl or dc),
        key=lambda o: (-distance(o[0], layers), o),
    )

    def peer1(step):
        y = lax.rem(chip_y + step[0], chips_y)
        return ((layer * 2 + lax.rem(y, 2)) * 2 + core, y // 2, lax.rem(gz + step[1], nz))

    def peer2(step):
        other = lax.rem(layer + step[0], layers)
        return ((other * 2 + low) * 2 + lax.rem(core + step[1], 2), gy, gz)

    far = core * 2
    near = 2 - far
    far_x = gx + far - 1
    has_far = jnp.logical_and(far_x >= 0, far_x < nx)
    far_device = (far_x, gy, gz)
    corner_device = (far_x, 1 - gy, gz)
    near_device = (gx + near - 1, gy, gz)
    side_device = (gx, 1 - gy, gz)
    has_z = (gz < nz - 1, gz > 0)
    from_z = (gz > 0, gz < nz - 1)
    halo_row = jnp.where(gy == 0, ROWS_Y - 1, 0)
    halo_step = jnp.where(gy == 0, 2, 0)

    barrier = pltpu.get_barrier_semaphore()

    def greet(device):
        pl.semaphore_signal(barrier, inc=1, device_id=device, device_id_type=MESH)

    for k in range(max(len(steps1), len(steps2))):
        if k < len(steps1):
            greet(peer1(steps1[k]))
        if k < len(steps2):
            greet(peer2(steps2[k]))

    @pl.when(has_far)
    def _():
        greet(far_device)
        greet(corner_device)

    greeted = n1 - 1 + n2 - 1 + jnp.where(has_far, 2, 0)

    field_copy = pltpu.make_async_copy(start_ref, field, ssem)

    def j_copy(order, cz):
        return pltpu.make_async_copy(j_ref.at[:, cz], jv.at[cz], jsem.at[order])

    cz_order = (0, 2, 1)
    codes_copy = pltpu.make_async_copy(codes_hbm, codes_ref, csem)
    codes_copy.start()
    j_copy(0, 0).start()
    field_copy.start()
    j_copy(1, 2).start()
    j_copy(2, 1).start()

    codes_copy.wait()
    codes = jnp.concatenate([codes_ref[cz] for cz in range(ROWS_Z)], axis=0)
    place = lax.broadcasted_iota(jnp.int32, codes.shape, 1)
    inverse = jnp.zeros_like(codes)
    for code in range(SLOTS):
        slot = jnp.max(jnp.where(codes == code, place, 0), axis=1, keepdims=True)
        inverse = jnp.where(place == code, slot, inverse)
    inv_vmem[...] = jnp.zeros_like(inv_vmem)
    inv_vmem[: ROWS_Y * ROWS_Z, :SLOTS] = inverse
    inv_copy = pltpu.make_async_copy(inv_vmem, inv_ref, isem)
    inv_copy.start()

    def send(source, target, send_sem, recv_sem, device):
        return pltpu.make_async_remote_copy(
            src_ref=source,
            dst_ref=target,
            send_sem=send_sem,
            recv_sem=recv_sem,
            device_id=device,
            device_id_type=MESH,
        )

    def near_copy(t, z):
        return send(push.at[t, near, z], near_buf.at[t, z], ns.at[t, z], nr.at[t, z], near_device)

    def z_device(way):
        return (gx, gy, gz + 1 if way == UP else gz - 1)

    def z_far_copy(t, way, y):
        return send(
            push.at[t, far, 4 if way == UP else 0, y],
            z_buf.at[t, way, 0, y],
            zs.at[t, way, y],
            zr.at[t, way, y],
            z_device(way),
        )

    def z_own_copy(t, way, part):
        rows = pl.ds(ROWS_Y, 1) if part == 0 else pl.ds(0, ROWS_Y)
        return send(
            push.at[t, 1, 4 if way == UP else 0, rows],
            z_buf.at[t, way, 1, rows],
            zos.at[t, way, part],
            zor.at[t, way, part],
            z_device(way),
        )

    def middle_copy(t):
        return send(
            push.at[t, far, 2, pl.ds(0, ROWS_Y)], far_buf.at[t, 1], ms.at[t], mr.at[t], far_device
        )

    def far_copy(t, z, y):
        return send(
            push.at[t, far, z, y],
            far_buf.at[t, z - 1, y],
            fs.at[t, z // 2, y],
            fr.at[t, z // 2, y],
            far_device,
        )

    def corner_copy(t):
        return send(
            push.at[t, far, pl.ds(1, ROWS_Z), ROWS_Y],
            corner_buf.at[t],
            cs.at[t],
            cr.at[t],
            corner_device,
        )

    def y_copy(t):
        return send(
            push.at[t, 1, pl.ds(1, ROWS_Z), ROWS_Y], y_buf.at[t], ys.at[t], yr.at[t], side_device
        )

    def gather_plane(t, dx, z):
        for y in range(ROWS_Y + 1):
            value = None
            for cz in range(max(0, z - 2), min(ROWS_Z - 1, z) + 1):
                oz = z - cz
                if y == ROWS_Y:
                    pairs = [(halo_row, halo_step)]
                else:
                    pairs = [
                        (b, y + 1 - b) for b in range(max(0, y - 1), min(ROWS_Y - 1, y + 1) + 1)
                    ]
                for b, oy in pairs:
                    term = prod[cz, b, inv_ref[cz * ROWS_Y + b, dx * 9 + oy * 3 + oz]]
                    value = term if value is None else value + term
            push[t, dx, z, y] = value

    def terms(value):
        high = value.astype(jnp.bfloat16)
        return high, (value - high.astype(jnp.float32)).astype(jnp.bfloat16)

    def multiply(t, cz):
        for half in range(ROWS_Y // 2):
            q = cz * 2 + half
            if t == 0:
                for column in range(0, SLOTS * WIDTH, 128):
                    size = min(128, SLOTS * WIDTH - column)
                    both = jnp.concatenate(
                        [
                            jv[cz, 2 * half, :, column : column + size],
                            jv[cz, 2 * half + 1, :, column : column + size],
                        ],
                        axis=0,
                    ).T
                    jt[q, column : column + size, :128] = both
                    jt[q, column : column + size, 128:] = both
            one = terms(source(t, 2 * half, cz))
            two = terms(source(t, 2 * half + 1, cz))
            none = jnp.zeros_like(one[0])
            weights = jnp.concatenate(
                [
                    jnp.concatenate(pair, axis=1)
                    for k in range(2)
                    for pair in ([one[k], none], [none, two[k]])
                ],
                axis=0,
            )
            for slot in range(0, SLOTS, TILE_SLOTS):
                out = jnp.dot(
                    jt[q, slot * WIDTH : (slot + TILE_SLOTS) * WIDTH, :],
                    weights,
                    preferred_element_type=jnp.float32,
                )
                tile = (TILE_SLOTS, WIDTH, RHS)
                prod[cz, 2 * half, slot : slot + TILE_SLOTS] = out[:, :RHS].reshape(tile)
                prod[cz, 2 * half + 1, slot : slot + TILE_SLOTS] = out[:, RHS:].reshape(tile)

    def wide(t, b, cz):
        return push[t, 1, cz + 1, b]

    def source(t, b, cz):
        return field[b, cz] if t == 0 else wide(0, b, cz)

    def apply(t, beside, later, last):
        met = []

        def out(action):
            if t == 0 and not met:
                met.append(True)
                pl.semaphore_wait(barrier, greeted)
            action()

        def out_z_far(way, rows=(0, ROWS_Y, 1)):
            @pl.when(has_z[way])
            def _():
                for y in rows:
                    z_far_copy(t, way, y).start()

        def out_middle():
            @pl.when(has_far)
            def _():
                middle_copy(t).start()

        if t == 1:
            beside()
        for order, cz in enumerate(cz_order):
            if t == 0:
                j_copy(order, cz).wait()
                if order == 0:
                    field_copy.wait()
            multiply(t, cz)
            if t == 0 and order == 0:
                inv_copy.wait()
            if cz == 1:
                continue
            way, z = (DOWN, 0) if cz == 0 else (UP, 4)
            gather_plane(t, far, z)
            out(functools.partial(out_z_far, way))

        gather_plane(t, far, 2)
        out(out_middle)
        for z in (0, 4, 2, 3, 1):
            gather_plane(t, near, z)
            out(near_copy(t, z).start)
        gather_plane(t, far, 3)
        gather_plane(t, far, 1)
        for z in (0, 4, 2, 3, 1):
            gather_plane(t, 1, z)
        for way, z in ((DOWN, 0), (UP, 4)):
            near_copy(t, z).wait_recv()
            push[t, 1, z] = push[t, 1, z] + near_buf[t, z]

            @pl.when(has_z[way])
            def _():
                z_own_copy(t, way, 0).start()

        for way in (DOWN, UP):
            out_z_far(way, (2, 3))

            @pl.when(has_z[way])
            def _():
                z_own_copy(t, way, 1).start()

        if t == 0:
            beside()
        for z in (2, 3, 1):
            near_copy(t, z).wait_recv()
            push[t, 1, z] = push[t, 1, z] + near_buf[t, z]

        def from_z_far(y):
            for way, z in ((DOWN, 3), (UP, 1)):

                @pl.when(from_z[way])
                def _():
                    z_far_copy(t, way, y).wait_recv()
                    push[t, far, z, y] = push[t, far, z, y] + z_buf[t, way, 0, y]

                if y < ROWS_Y:

                    @pl.when(has_far)
                    def _():
                        far_copy(t, z, y).start()

        def from_z_own(part):
            rows = slice(ROWS_Y, ROWS_Y + 1) if part == 0 else slice(0, ROWS_Y)
            for way, z in ((DOWN, 3), (UP, 1)):

                @pl.when(from_z[way])
                def _():
                    z_own_copy(t, way, part).wait_recv()
                    push[t, 1, z, rows] = push[t, 1, z, rows] + z_buf[t, way, 1, rows]

        def from_far(y):
            @pl.when(has_far)
            def _():
                for z in (3, 1):
                    far_copy(t, z, y).wait_recv()
                    push[t, 1, z, y] = push[t, 1, z, y] + far_buf[t, z - 1, y]

        from_z_far(0)
        from_z_far(ROWS_Y)

        @pl.when(has_far)
        def _():
            corner_copy(t).start()

        from_z_far(1)
        from_z_own(0)
        y_copy(t).start()
        from_z_far(2)
        from_z_far(3)
        later()
        from_z_own(1)

        @pl.when(has_far)
        def _():
            middle_copy(t).wait_recv()
            push[t, 1, 2, :ROWS_Y] = push[t, 1, 2, :ROWS_Y] + far_buf[t, 1]

        from_far(0)

        @pl.when(has_far)
        def _():
            corner_copy(t).wait_recv()
            for z in range(ROWS_Z):
                push[t, 1, z + 1, halo_row] = push[t, 1, z + 1, halo_row] + corner_buf[t, z]

        from_far(1)
        y_copy(t).wait_recv()
        for z in range(ROWS_Z):
            push[t, 1, z + 1, halo_row] = push[t, 1, z + 1, halo_row] + y_buf[t, z]
        from_far(2)
        last()
        from_far(3)

    def finish(t):
        for way in (UP, DOWN):

            @pl.when(has_z[way])
            def _():
                for y in range(ROWS_Y + 1):
                    z_far_copy(t, way, y).wait_send()
                for part in (0, 1):
                    z_own_copy(t, way, part).wait_send()

        for z in range(ROWS_Z + 2):
            near_copy(t, z).wait_send()

        @pl.when(has_far)
        def _():
            middle_copy(t).wait_send()
            corner_copy(t).wait_send()
            for y in range(ROWS_Y):
                for z in (3, 1):
                    far_copy(t, z, y).wait_send()

        y_copy(t).wait_send()

    cells = [(b, cz) for b in range(ROWS_Y) for cz in range(ROWS_Z)]

    def summed(terms):
        acc = None
        for term in terms:
            acc = term if acc is None else acc + term
        return jnp.sum(acc, axis=0, keepdims=True)

    stages = ((plane_buf, me1, peer1, steps1), (line_buf, me2, peer2, steps2))

    def exchange_start(t, stage):
        buf, me, peer, steps = stages[stage]
        for step in steps:
            send(
                buf.at[t, me], buf.at[t, me], gs.at[t, stage], gr.at[t, stage], peer(step)
            ).start()

    def exchange_end(t, stage):
        buf, me, peer, steps = stages[stage]
        every = buf.at[t, pl.ds(0, len(steps))]
        copy = send(every, every, gs.at[t, stage], gr.at[t, stage], peer(steps[0]))
        copy.wait_send()
        copy.wait_recv()
        return rows_of(buf[t])

    def put(buf, t, me, rows):
        blank = [jnp.zeros((1, RHS), jnp.float32)] * (8 - len(rows))
        buf[t, me] = jnp.concatenate(list(rows) + blank, axis=0)

    squares = []

    def first_squares():
        squares.append(summed(field[b, cz] * field[b, cz] for b, cz in cells))

    def first_sums():
        g = squares[0]
        a = summed(wide(0, b, cz) * field[b, cz] for b, cz in cells)
        c = divided(a, g)
        r = summed((wide(0, b, cz) - c * field[b, cz]) ** 2 for b, cz in cells)
        e = summed((wide(0, b, cz) - c * field[b, cz]) * field[b, cz] for b, cz in cells)
        put(plane_buf, 0, me1, (g, c, r, e))
        exchange_start(0, 0)

    def first_layer():
        rows = exchange_end(0, 0)
        put(line_buf, 0, me2, merged_one(*rows[:4])[:4])
        exchange_start(0, 1)

    def nothing():
        pass

    found = []

    def first_end():
        g, c, r, e, a = merged_one(*exchange_end(0, 1)[:4])
        scale_square = g / entries + epsilon
        coef_one = a / entries / scale_square
        d = c - coef_one
        r = jnp.maximum(r + d * (2.0 * e + d * g), 0.0)
        norm_one = jnp.sqrt(r / entries / scale_square + epsilon)
        inv_scale = 1.0 / jnp.sqrt(scale_square)
        inv_second = 1.0 / norm_one
        for b, cz in cells:
            first = field[b, cz] * inv_scale
            wide_one = wide(0, b, cz) * inv_scale
            field[b, cz] = first
            second[b, cz] = (wide_one - coef_one * first) * inv_second
        g11 = summed(field[b, cz] * field[b, cz] for b, cz in cells)
        g12 = summed(field[b, cz] * second[b, cz] for b, cz in cells)
        g22 = summed(second[b, cz] * second[b, cz] for b, cz in cells)
        found.extend(
            (coef_one, norm_one, inv_scale * inv_second, coef_one * inv_scale * inv_second)
        )
        found.extend((g11, g12, g22))

    apply(0, first_squares, nothing, nothing)
    apply(1, first_sums, first_layer, first_end)
    coef_one, norm_one, gain, shift, g11, g12, g22 = found

    for b, cz in cells:
        image[b, cz] = wide(1, b, cz) * gain - wide(0, b, cz) * shift
    a1 = summed(image[b, cz] * field[b, cz] for b, cz in cells)
    a2 = summed(image[b, cz] * second[b, cz] for b, cz in cells)
    c1, c2 = fitted(g11, g12, g22, a1, a2)
    for b, cz in cells:
        rest_ref[b, cz] = image[b, cz] - c1 * field[b, cz] - c2 * second[b, cz]
    r = summed(rest_ref[b, cz] * rest_ref[b, cz] for b, cz in cells)
    e1 = summed(rest_ref[b, cz] * field[b, cz] for b, cz in cells)
    e2 = summed(rest_ref[b, cz] * second[b, cz] for b, cz in cells)
    put(plane_buf, 1, me1, (g11, g12, g22, c1, c2, r, e1, e2))
    exchange_start(1, 0)
    put(line_buf, 1, me2, merged_two(*exchange_end(1, 0))[:8])
    exchange_start(1, 1)
    finish(0)
    finish(1)
    g11, g12, g22, c1, c2, r, e1, e2, a1, a2 = merged_two(*exchange_end(1, 1))
    coef_two = a1 / entries
    coef_three = a2 / entries
    d1, d2 = c1 - coef_two, c2 - coef_three
    p1 = d1 * g11 + d2 * g12
    p2 = d1 * g12 + d2 * g22
    r = jnp.maximum(r + d1 * (2.0 * e1 + p1) + d2 * (2.0 * e2 + p2), 0.0)
    norm_two = jnp.sqrt(r / entries + epsilon)
    for b, cz in cells:
        rest_ref[b, cz] = image[b, cz] - coef_two * field[b, cz] - coef_three * second[b, cz]
    hess_ref[...] = jnp.concatenate(
        [coef_one, norm_one, coef_two, coef_three, norm_two, norm_two, norm_two, norm_two], axis=0
    )


def per_device(nx, ny, nz, jacobian, columns, start, velocity, design, mask):
    n1 = nz * ny * 2
    n2 = nx // 2
    codes = jnp.transpose(columns, (0, 2, 1, 3)).reshape(ROWS_Z, ROWS_Y, SLOTS)
    block = (WIDTH, RHS)
    f32 = jnp.float32
    rest, hess = pl.pallas_call(
        functools.partial(kernel, nx, ny, nz),
        out_shape=(
            jax.ShapeDtypeStruct((ROWS_Y, ROWS_Z) + block, f32),
            jax.ShapeDtypeStruct((8, RHS), f32),
        ),
        in_specs=[
            pl.BlockSpec(memory_space=pltpu.HBM),
            pl.BlockSpec(memory_space=pltpu.HBM),
            pl.BlockSpec(memory_space=pltpu.HBM),
        ],
        out_specs=(
            pl.BlockSpec(memory_space=pltpu.VMEM),
            pl.BlockSpec(memory_space=pltpu.VMEM),
        ),
        scratch_shapes=[
            pltpu.VMEM((ROWS_Z, ROWS_Y, SLOTS), jnp.int32),
            pltpu.VMEM((16, 128), jnp.int32),
            pltpu.SMEM((16, 128), jnp.int32),
            pltpu.VMEM((ROWS_Z, ROWS_Y, WIDTH, SLOTS * WIDTH), jnp.bfloat16),
            pltpu.VMEM((ROWS_Z * ROWS_Y // 2, SLOTS * WIDTH, 4 * WIDTH), jnp.bfloat16),
            pltpu.VMEM((ROWS_Z, ROWS_Y, SLOTS) + block, f32),
            pltpu.VMEM((2, 3, ROWS_Z + 2, ROWS_Y + 1) + block, f32),
            pltpu.VMEM((2, ROWS_Z + 2, ROWS_Y + 1) + block, f32),
            pltpu.VMEM((2, 2, 2, ROWS_Y + 1) + block, f32),
            pltpu.VMEM((2, ROWS_Z, ROWS_Y) + block, f32),
            pltpu.VMEM((2, ROWS_Z) + block, f32),
            pltpu.VMEM((2, ROWS_Z) + block, f32),
            pltpu.VMEM((ROWS_Y, ROWS_Z) + block, f32),
            pltpu.VMEM((ROWS_Y, ROWS_Z) + block, f32),
            pltpu.VMEM((ROWS_Y, ROWS_Z) + block, f32),
            pltpu.VMEM((2, n1, 8, RHS), f32),
            pltpu.VMEM((2, n2, 8, RHS), f32),
            pltpu.SemaphoreType.DMA,
            pltpu.SemaphoreType.DMA,
            pltpu.SemaphoreType.DMA((3,)),
            pltpu.SemaphoreType.DMA,
            pltpu.SemaphoreType.DMA((2, ROWS_Z + 2)),
            pltpu.SemaphoreType.DMA((2, ROWS_Z + 2)),
            pltpu.SemaphoreType.DMA((2, 2, ROWS_Y + 1)),
            pltpu.SemaphoreType.DMA((2, 2, ROWS_Y + 1)),
            pltpu.SemaphoreType.DMA((2, 2, 2)),
            pltpu.SemaphoreType.DMA((2, 2, 2)),
            pltpu.SemaphoreType.DMA((2,)),
            pltpu.SemaphoreType.DMA((2,)),
            pltpu.SemaphoreType.DMA((2, 2, ROWS_Y)),
            pltpu.SemaphoreType.DMA((2, 2, ROWS_Y)),
            pltpu.SemaphoreType.DMA((2,)),
            pltpu.SemaphoreType.DMA((2,)),
            pltpu.SemaphoreType.DMA((2,)),
            pltpu.SemaphoreType.DMA((2,)),
            pltpu.SemaphoreType.DMA((2, 2)),
            pltpu.SemaphoreType.DMA((2, 2)),
        ],
        compiler_params=pltpu.CompilerParams(
            collective_id=0, has_side_effects=True, vmem_limit_bytes=52 * 1024 * 1024
        ),
    )(
        pltpu.with_memory_space_constraint(codes, pltpu.HBM),
        jacobian.reshape(ROWS_Y, ROWS_Z, WIDTH, SLOTS * WIDTH),
        pltpu.with_memory_space_constraint(start.reshape((ROWS_Y, ROWS_Z) + block), pltpu.HBM),
    )
    hessenberg = hess[:5]
    adjoint = (rest / hess[4]).reshape(start.shape)
    cells = design.shape[3]
    shaped = adjoint.reshape(adjoint.shape[:3] + (WIDTH // cells, cells, RHS))
    dotted = jnp.sum(velocity[..., None] * shaped[:, :, :, 0:3], axis=3)
    slope = -0.11 / ((0.1 + design) * (0.1 + design))
    sensitivity = (mask.astype(f32) * slope)[..., None] * dotted
    return (adjoint, hessenberg, sensitivity)


def solution(mesh):
    shape = mesh.shape
    in_specs = (
        P("gx", "gy", "gz", None, None),
        P("gx", "gy", "gz", None),
        P("gx", "gy", "gz", None, None),
        P("gx", "gy", "gz", None, None),
        P("gx", "gy", "gz", None),
        P("gx", "gy", "gz", None),
    )
    out_specs = (P("gx", "gy", "gz", None, None), P(), P("gx", "gy", "gz", None, None))
    return jax.shard_map(
        functools.partial(per_device, shape["gx"], shape["gy"], shape["gz"]),
        mesh=mesh,
        in_specs=in_specs,
        out_specs=out_specs,
        check_vma=False,
    )
```

```python
import functools

import jax
import jax.numpy as jnp
from jax import lax
from jax.experimental import pallas as pl
from jax.experimental.pallas import tpu as pltpu
from jax.sharding import PartitionSpec as P

MESH = pl.DeviceIdType.MESH
epsilon = 1e-06
SLOTS = 27
WIDTH = 64
RHS = 128
ROWS_Y = 4
ROWS_Z = 3
TILE_SLOTS = 9
UP, DOWN = 0, 1


def divided(value, by):
    safe = by > 0
    return jnp.where(safe, value / jnp.where(safe, by, 1.0), 0.0)


def fitted(g11, g12, g22, a1, a2):
    det = g11 * g22 - g12 * g12
    good = det > 1e-4 * g11 * g22
    c2 = jnp.where(good, (g11 * a2 - g12 * a1) / jnp.where(good, det, 1.0), 0.0)
    return divided(a1 - g12 * c2, g11), c2


def total(value):
    return jnp.sum(value, axis=0)


def merged_one(g, c, r, e):
    whole = total(g)
    inner = total(g * c + e)
    centre = divided(inner, whole)
    d = c - centre
    return whole, centre, total(r + d * (2.0 * e + d * g)), total(e + d * g), inner


def merged_two(g11, g12, g22, c1, c2, r, e1, e2):
    w11, w12, w22 = total(g11), total(g12), total(g22)
    a1 = total(g11 * c1 + g12 * c2 + e1)
    a2 = total(g12 * c1 + g22 * c2 + e2)
    k1, k2 = fitted(w11, w12, w22, a1, a2)
    d1, d2 = c1 - k1, c2 - k2
    p1 = d1 * g11 + d2 * g12
    p2 = d1 * g12 + d2 * g22
    rest = total(r + d1 * (2.0 * e1 + p1) + d2 * (2.0 * e2 + p2))
    return w11, w12, w22, k1, k2, rest, total(e1 + p1), total(e2 + p2), a1, a2


def rows_of(block):
    return [block[:, k : k + 1, :] for k in range(8)]


def kernel(
    nx, ny, nz,
    codes_hbm, j_ref, start_ref,
    rest_ref, hess_ref,
    codes_ref, inv_vmem, inv_ref, jv, jt, prod, push, near_buf, z_buf, far_buf, corner_buf, y_buf, field, second, image, plane_buf, line_buf,
    csem, isem, jsem, ssem, ns, nr, zs, zr, zos, zor, ms, mr, fs, fr, cs, cr, ys, yr, gs, gr,
):
    gx = lax.axis_index("gx")
    gy = lax.axis_index("gy")
    gz = lax.axis_index("gz")
    entries = float(nx * ny * nz * ROWS_Y * ROWS_Z * WIDTH)

    layers = nx // 4
    layer = gx // 4
    low = lax.rem(gx // 2, 2)
    core = lax.rem(gx, 2)
    chip_y = gy * 2 + low
    chips_y = ny * 2

    def distance(step, size):
        return min(step, size - step)

    n1, me1 = chips_y * nz, chip_y * nz + gz
    n2, me2 = layers * 2, layer * 2 + core
    steps1 = sorted(
        ((dy, dz) for dy in range(chips_y) for dz in range(nz) if dy or dz),
        key=lambda o: (-distance(o[0], chips_y) - distance(o[1], nz), o),
    )
    steps2 = sorted(
        ((dl, dc) for dl in range(layers) for dc in range(2) if dl or dc),
        key=lambda o: (-distance(o[0], layers), o),
    )

    def peer1(step):
        y = lax.rem(chip_y + step[0], chips_y)
        return ((layer * 2 + lax.rem(y, 2)) * 2 + core, y // 2, lax.rem(gz + step[1], nz))

    def peer2(step):
        other = lax.rem(layer + step[0], layers)
        return ((other * 2 + low) * 2 + lax.rem(core + step[1], 2), gy, gz)

    far = core * 2
    near = 2 - far
    far_x = gx + far - 1
    has_far = jnp.logical_and(far_x >= 0, far_x < nx)
    far_device = (far_x, gy, gz)
    corner_device = (far_x, 1 - gy, gz)
    near_device = (gx + near - 1, gy, gz)
    side_device = (gx, 1 - gy, gz)
    has_z = (gz < nz - 1, gz > 0)
    from_z = (gz > 0, gz < nz - 1)
    halo_row = jnp.where(gy == 0, ROWS_Y - 1, 0)
    halo_step = jnp.where(gy == 0, 2, 0)

    barrier = pltpu.get_barrier_semaphore()

    def greet(device):
        pl.semaphore_signal(barrier, inc=1, device_id=device, device_id_type=MESH)

    for k in range(max(len(steps1), len(steps2))):
        if k < len(steps1):
            greet(peer1(steps1[k]))
        if k < len(steps2):
            greet(peer2(steps2[k]))

    @pl.when(has_far)
    def _():
        greet(far_device)
        greet(corner_device)

    greeted = n1 - 1 + n2 - 1 + jnp.where(has_far, 2, 0)

    field_copy = pltpu.make_async_copy(start_ref, field, ssem)

    def j_copy(order, cz):
        return pltpu.make_async_copy(j_ref.at[:, cz], jv.at[cz], jsem.at[order])

    cz_order = (0, 2, 1)
    codes_copy = pltpu.make_async_copy(codes_hbm, codes_ref, csem)
    codes_copy.start()
    j_copy(0, 0).start()
    field_copy.start()
    j_copy(1, 2).start()
    j_copy(2, 1).start()

    codes_copy.wait()
    codes = jnp.concatenate([codes_ref[cz] for cz in range(ROWS_Z)], axis=0)
    place = lax.broadcasted_iota(jnp.int32, codes.shape, 1)
    inverse = jnp.zeros_like(codes)
    for code in range(SLOTS):
        slot = jnp.max(jnp.where(codes == code, place, 0), axis=1, keepdims=True)
        inverse = jnp.where(place == code, slot, inverse)
    inv_vmem[...] = jnp.zeros_like(inv_vmem)
    inv_vmem[: ROWS_Y * ROWS_Z, :SLOTS] = inverse
    inv_copy = pltpu.make_async_copy(inv_vmem, inv_ref, isem)
    inv_copy.start()

    def send(source, target, send_sem, recv_sem, device):
        return pltpu.make_async_remote_copy(
            src_ref=source,
            dst_ref=target,
            send_sem=send_sem,
            recv_sem=recv_sem,
            device_id=device,
            device_id_type=MESH,
        )

    def near_copy(t, z):
        return send(push.at[t, near, z], near_buf.at[t, z], ns.at[t, z], nr.at[t, z], near_device)

    def z_device(way):
        return (gx, gy, gz + 1 if way == UP else gz - 1)

    def z_far_copy(t, way, y):
        return send(
            push.at[t, far, 4 if way == UP else 0, y],
            z_buf.at[t, way, 0, y],
            zs.at[t, way, y],
            zr.at[t, way, y],
            z_device(way),
        )

    def z_own_copy(t, way, part):
        rows = pl.ds(ROWS_Y, 1) if part == 0 else pl.ds(0, ROWS_Y)
        return send(
            push.at[t, 1, 4 if way == UP else 0, rows],
            z_buf.at[t, way, 1, rows],
            zos.at[t, way, part],
            zor.at[t, way, part],
            z_device(way),
        )

    def middle_copy(t):
        return send(
            push.at[t, far, 2, pl.ds(0, ROWS_Y)], far_buf.at[t, 1], ms.at[t], mr.at[t], far_device
        )

    def far_copy(t, z, y):
        return send(
            push.at[t, far, z, y],
            far_buf.at[t, z - 1, y],
            fs.at[t, z // 2, y],
            fr.at[t, z // 2, y],
            far_device,
        )

    def corner_copy(t):
        return send(
            push.at[t, far, pl.ds(1, ROWS_Z), ROWS_Y],
            corner_buf.at[t],
            cs.at[t],
            cr.at[t],
            corner_device,
        )

    def y_copy(t):
        return send(
            push.at[t, 1, pl.ds(1, ROWS_Z), ROWS_Y], y_buf.at[t], ys.at[t], yr.at[t], side_device
        )

    def gather_plane(t, dx, z):
        for y in range(ROWS_Y + 1):
            value = None
            for cz in range(max(0, z - 2), min(ROWS_Z - 1, z) + 1):
                oz = z - cz
                if y == ROWS_Y:
                    pairs = [(halo_row, halo_step)]
                else:
                    pairs = [
                        (b, y + 1 - b) for b in range(max(0, y - 1), min(ROWS_Y - 1, y + 1) + 1)
                    ]
                for b, oy in pairs:
                    term = prod[cz, b, inv_ref[cz * ROWS_Y + b, dx * 9 + oy * 3 + oz]]
                    value = term if value is None else value + term
            push[t, dx, z, y] = value

    def terms(value):
        high = value.astype(jnp.bfloat16)
        return high, (value - high.astype(jnp.float32)).astype(jnp.bfloat16)

    def multiply(t, cz):
        for half in range(ROWS_Y // 2):
            q = cz * 2 + half
            if t == 0:
                for column in range(0, SLOTS * WIDTH, 128):
                    size = min(128, SLOTS * WIDTH - column)
                    both = jnp.concatenate(
                        [
                            jv[cz, 2 * half, :, column : column + size],
                            jv[cz, 2 * half + 1, :, column : column + size],
                        ],
                        axis=0,
                    ).T
                    jt[q, column : column + size, :128] = both
                    jt[q, column : column + size, 128:] = both
            one = terms(source(t, 2 * half, cz))
            two = terms(source(t, 2 * half + 1, cz))
            none = jnp.zeros_like(one[0])
            weights = jnp.concatenate(
                [
                    jnp.concatenate(pair, axis=1)
                    for k in range(2)
                    for pair in ([one[k], none], [none, two[k]])
                ],
                axis=0,
            )
            for slot in range(0, SLOTS, TILE_SLOTS):
                out = jnp.dot(
                    jt[q, slot * WIDTH : (slot + TILE_SLOTS) * WIDTH, :],
                    weights,
                    preferred_element_type=jnp.float32,
                )
                tile = (TILE_SLOTS, WIDTH, RHS)
                prod[cz, 2 * half, slot : slot + TILE_SLOTS] = out[:, :RHS].reshape(tile)
                prod[cz, 2 * half + 1, slot : slot + TILE_SLOTS] = out[:, RHS:].reshape(tile)

    def wide(t, b, cz):
        return push[t, 1, cz + 1, b]

    def source(t, b, cz):
        return field[b, cz] if t == 0 else wide(0, b, cz)

    def apply(t, beside, later, last):
        met = []

        def out(action):
            if t == 0 and not met:
                met.append(True)
                pl.semaphore_wait(barrier, greeted)
            action()

        def out_z_far(way, rows=(0, ROWS_Y, 1)):
            @pl.when(has_z[way])
            def _():
                for y in rows:
                    z_far_copy(t, way, y).start()

        def out_middle():
            @pl.when(has_far)
            def _():
                middle_copy(t).start()

        if t == 1:
            beside()
        for order, cz in enumerate(cz_order):
            if t == 0:
                j_copy(order, cz).wait()
                if order == 0:
                    field_copy.wait()
            multiply(t, cz)
            if t == 0 and order == 0:
                inv_copy.wait()
            if cz == 1:
                continue
            way, z = (DOWN, 0) if cz == 0 else (UP, 4)
            gather_plane(t, far, z)
            out(functools.partial(out_z_far, way))

        gather_plane(t, far, 2)
        out(out_middle)
        for z in (0, 4, 2, 3, 1):
            gather_plane(t, near, z)
            out(near_copy(t, z).start)
        gather_plane(t, far, 3)
        gather_plane(t, far, 1)
        for z in (0, 4, 2, 3, 1):
            gather_plane(t, 1, z)
        for way, z in ((DOWN, 0), (UP, 4)):
            near_copy(t, z).wait_recv()
            push[t, 1, z] = push[t, 1, z] + near_buf[t, z]

            @pl.when(has_z[way])
            def _():
                z_own_copy(t, way, 0).start()

        for way in (DOWN, UP):
            out_z_far(way, (2, 3))

            @pl.when(has_z[way])
            def _():
                z_own_copy(t, way, 1).start()

        if t == 0:
            beside()
        for z in (2, 3, 1):
            near_copy(t, z).wait_recv()
            push[t, 1, z] = push[t, 1, z] + near_buf[t, z]

        def from_z_far(y):
            for way, z in ((DOWN, 3), (UP, 1)):

                @pl.when(from_z[way])
                def _():
                    z_far_copy(t, way, y).wait_recv()
                    push[t, far, z, y] = push[t, far, z, y] + z_buf[t, way, 0, y]

                if y < ROWS_Y:

                    @pl.when(has_far)
                    def _():
                        far_copy(t, z, y).start()

        def from_z_own(part):
            rows = slice(ROWS_Y, ROWS_Y + 1) if part == 0 else slice(0, ROWS_Y)
            for way, z in ((DOWN, 3), (UP, 1)):

                @pl.when(from_z[way])
                def _():
                    z_own_copy(t, way, part).wait_recv()
                    push[t, 1, z, rows] = push[t, 1, z, rows] + z_buf[t, way, 1, rows]

        def from_far(y):
            @pl.when(has_far)
            def _():
                for z in (3, 1):
                    far_copy(t, z, y).wait_recv()
                    push[t, 1, z, y] = push[t, 1, z, y] + far_buf[t, z - 1, y]

        from_z_far(0)
        from_z_far(ROWS_Y)

        @pl.when(has_far)
        def _():
            corner_copy(t).start()

        from_z_far(1)
        from_z_own(0)
        y_copy(t).start()
        from_z_far(2)
        later()
        from_z_far(3)
        from_z_own(1)

        @pl.when(has_far)
        def _():
            middle_copy(t).wait_recv()
            push[t, 1, 2, :ROWS_Y] = push[t, 1, 2, :ROWS_Y] + far_buf[t, 1]

        from_far(0)

        @pl.when(has_far)
        def _():
            corner_copy(t).wait_recv()
            for z in range(ROWS_Z):
                push[t, 1, z + 1, halo_row] = push[t, 1, z + 1, halo_row] + corner_buf[t, z]

        from_far(1)
        y_copy(t).wait_recv()
        for z in range(ROWS_Z):
            push[t, 1, z + 1, halo_row] = push[t, 1, z + 1, halo_row] + y_buf[t, z]
        from_far(2)
        last()
        from_far(3)

    def finish(t):
        for way in (UP, DOWN):

            @pl.when(has_z[way])
            def _():
                for y in range(ROWS_Y + 1):
                    z_far_copy(t, way, y).wait_send()
                for part in (0, 1):
                    z_own_copy(t, way, part).wait_send()

        for z in range(ROWS_Z + 2):
            near_copy(t, z).wait_send()

        @pl.when(has_far)
        def _():
            middle_copy(t).wait_send()
            corner_copy(t).wait_send()
            for y in range(ROWS_Y):
                for z in (3, 1):
                    far_copy(t, z, y).wait_send()

        y_copy(t).wait_send()

    cells = [(b, cz) for b in range(ROWS_Y) for cz in range(ROWS_Z)]

    def summed(terms):
        acc = None
        for term in terms:
            acc = term if acc is None else acc + term
        return jnp.sum(acc, axis=0, keepdims=True)

    stages = ((plane_buf, me1, peer1, steps1), (line_buf, me2, peer2, steps2))

    def exchange_start(t, stage):
        buf, me, peer, steps = stages[stage]
        for step in steps:
            send(
                buf.at[t, me], buf.at[t, me], gs.at[t, stage], gr.at[t, stage], peer(step)
            ).start()

    def exchange_whole(t, stage):
        buf, me, peer, steps = stages[stage]
        every = buf.at[t, pl.ds(0, len(steps))]
        return send(every, every, gs.at[t, stage], gr.at[t, stage], peer(steps[0]))

    def exchange_end(t, stage):
        exchange_whole(t, stage).wait_recv()
        return rows_of(stages[stage][0][t])

    def put(buf, t, me, rows):
        blank = [jnp.zeros((1, RHS), jnp.float32)] * (8 - len(rows))
        buf[t, me] = jnp.concatenate(list(rows) + blank, axis=0)

    squares = []

    def first_squares():
        squares.append(summed(field[b, cz] * field[b, cz] for b, cz in cells))

    def first_sums():
        g = squares[0]
        a = summed(wide(0, b, cz) * field[b, cz] for b, cz in cells)
        c = divided(a, g)
        r = summed((wide(0, b, cz) - c * field[b, cz]) ** 2 for b, cz in cells)
        e = summed((wide(0, b, cz) - c * field[b, cz]) * field[b, cz] for b, cz in cells)
        put(plane_buf, 0, me1, (g, c, r, e))
        exchange_start(0, 0)

    def first_layer():
        rows = exchange_end(0, 0)
        put(line_buf, 0, me2, merged_one(*rows[:4])[:4])
        exchange_start(0, 1)

    def nothing():
        pass

    found = []

    def first_end():
        g, c, r, e, a = merged_one(*exchange_end(0, 1)[:4])
        scale_square = g / entries + epsilon
        coef_one = a / entries / scale_square
        d = c - coef_one
        r = jnp.maximum(r + d * (2.0 * e + d * g), 0.0)
        norm_one = jnp.sqrt(r / entries / scale_square + epsilon)
        inv_scale = 1.0 / jnp.sqrt(scale_square)
        inv_second = 1.0 / norm_one
        for b, cz in cells:
            first = field[b, cz] * inv_scale
            wide_one = wide(0, b, cz) * inv_scale
            field[b, cz] = first
            second[b, cz] = (wide_one - coef_one * first) * inv_second
        g11 = summed(field[b, cz] * field[b, cz] for b, cz in cells)
        g12 = summed(field[b, cz] * second[b, cz] for b, cz in cells)
        g22 = summed(second[b, cz] * second[b, cz] for b, cz in cells)
        found.extend(
            (coef_one, norm_one, inv_scale * inv_second, coef_one * inv_scale * inv_second)
        )
        found.extend((g11, g12, g22))

    apply(0, first_squares, nothing, nothing)
    apply(1, first_sums, first_layer, first_end)
    coef_one, norm_one, gain, shift, g11, g12, g22 = found

    for b, cz in cells:
        image[b, cz] = wide(1, b, cz) * gain - wide(0, b, cz) * shift
    a1 = summed(image[b, cz] * field[b, cz] for b, cz in cells)
    a2 = summed(image[b, cz] * second[b, cz] for b, cz in cells)
    c1, c2 = fitted(g11, g12, g22, a1, a2)
    for b, cz in cells:
        rest_ref[b, cz] = image[b, cz] - c1 * field[b, cz] - c2 * second[b, cz]
    r = summed(rest_ref[b, cz] * rest_ref[b, cz] for b, cz in cells)
    e1 = summed(rest_ref[b, cz] * field[b, cz] for b, cz in cells)
    e2 = summed(rest_ref[b, cz] * second[b, cz] for b, cz in cells)
    put(plane_buf, 1, me1, (g11, g12, g22, c1, c2, r, e1, e2))
    exchange_start(1, 0)
    put(line_buf, 1, me2, merged_two(*exchange_end(1, 0))[:8])
    exchange_start(1, 1)
    finish(0)
    finish(1)
    for t, stage in ((0, 0), (0, 1), (1, 0)):
        exchange_whole(t, stage).wait_send()
    g11, g12, g22, c1, c2, r, e1, e2, a1, a2 = merged_two(*exchange_end(1, 1))
    coef_two = a1 / entries
    coef_three = a2 / entries
    d1, d2 = c1 - coef_two, c2 - coef_three
    p1 = d1 * g11 + d2 * g12
    p2 = d1 * g12 + d2 * g22
    r = jnp.maximum(r + d1 * (2.0 * e1 + p1) + d2 * (2.0 * e2 + p2), 0.0)
    norm_two = jnp.sqrt(r / entries + epsilon)
    for b, cz in cells:
        rest_ref[b, cz] = image[b, cz] - coef_two * field[b, cz] - coef_three * second[b, cz]
    hess_ref[...] = jnp.concatenate(
        [coef_one, norm_one, coef_two, coef_three, norm_two, norm_two, norm_two, norm_two], axis=0
    )
    exchange_whole(1, 1).wait_send()


def per_device(nx, ny, nz, jacobian, columns, start, velocity, design, mask):
    n1 = nz * ny * 2
    n2 = nx // 2
    codes = jnp.transpose(columns, (0, 2, 1, 3)).reshape(ROWS_Z, ROWS_Y, SLOTS)
    block = (WIDTH, RHS)
    f32 = jnp.float32
    rest, hess = pl.pallas_call(
        functools.partial(kernel, nx, ny, nz),
        out_shape=(
            jax.ShapeDtypeStruct((ROWS_Y, ROWS_Z) + block, f32),
            jax.ShapeDtypeStruct((8, RHS), f32),
        ),
        in_specs=[
            pl.BlockSpec(memory_space=pltpu.HBM),
            pl.BlockSpec(memory_space=pltpu.HBM),
            pl.BlockSpec(memory_space=pltpu.HBM),
        ],
        out_specs=(
            pl.BlockSpec(memory_space=pltpu.VMEM),
            pl.BlockSpec(memory_space=pltpu.VMEM),
        ),
        scratch_shapes=[
            pltpu.VMEM((ROWS_Z, ROWS_Y, SLOTS), jnp.int32),
            pltpu.VMEM((16, 128), jnp.int32),
            pltpu.SMEM((16, 128), jnp.int32),
            pltpu.VMEM((ROWS_Z, ROWS_Y, WIDTH, SLOTS * WIDTH), jnp.bfloat16),
            pltpu.VMEM((ROWS_Z * ROWS_Y // 2, SLOTS * WIDTH, 4 * WIDTH), jnp.bfloat16),
            pltpu.VMEM((ROWS_Z, ROWS_Y, SLOTS) + block, f32),
            pltpu.VMEM((2, 3, ROWS_Z + 2, ROWS_Y + 1) + block, f32),
            pltpu.VMEM((2, ROWS_Z + 2, ROWS_Y + 1) + block, f32),
            pltpu.VMEM((2, 2, 2, ROWS_Y + 1) + block, f32),
            pltpu.VMEM((2, ROWS_Z, ROWS_Y) + block, f32),
            pltpu.VMEM((2, ROWS_Z) + block, f32),
            pltpu.VMEM((2, ROWS_Z) + block, f32),
            pltpu.VMEM((ROWS_Y, ROWS_Z) + block, f32),
            pltpu.VMEM((ROWS_Y, ROWS_Z) + block, f32),
            pltpu.VMEM((ROWS_Y, ROWS_Z) + block, f32),
            pltpu.VMEM((2, n1, 8, RHS), f32),
            pltpu.VMEM((2, n2, 8, RHS), f32),
            pltpu.SemaphoreType.DMA,
            pltpu.SemaphoreType.DMA,
            pltpu.SemaphoreType.DMA((3,)),
            pltpu.SemaphoreType.DMA,
            pltpu.SemaphoreType.DMA((2, ROWS_Z + 2)),
            pltpu.SemaphoreType.DMA((2, ROWS_Z + 2)),
            pltpu.SemaphoreType.DMA((2, 2, ROWS_Y + 1)),
            pltpu.SemaphoreType.DMA((2, 2, ROWS_Y + 1)),
            pltpu.SemaphoreType.DMA((2, 2, 2)),
            pltpu.SemaphoreType.DMA((2, 2, 2)),
            pltpu.SemaphoreType.DMA((2,)),
            pltpu.SemaphoreType.DMA((2,)),
            pltpu.SemaphoreType.DMA((2, 2, ROWS_Y)),
            pltpu.SemaphoreType.DMA((2, 2, ROWS_Y)),
            pltpu.SemaphoreType.DMA((2,)),
            pltpu.SemaphoreType.DMA((2,)),
            pltpu.SemaphoreType.DMA((2,)),
            pltpu.SemaphoreType.DMA((2,)),
            pltpu.SemaphoreType.DMA((2, 2)),
            pltpu.SemaphoreType.DMA((2, 2)),
        ],
        compiler_params=pltpu.CompilerParams(
            collective_id=0, has_side_effects=True, vmem_limit_bytes=52 * 1024 * 1024
        ),
    )(
        pltpu.with_memory_space_constraint(codes, pltpu.HBM),
        jacobian.reshape(ROWS_Y, ROWS_Z, WIDTH, SLOTS * WIDTH),
        pltpu.with_memory_space_constraint(start.reshape((ROWS_Y, ROWS_Z) + block), pltpu.HBM),
    )
    hessenberg = hess[:5]
    adjoint = (rest / hess[4]).reshape(start.shape)
    cells = design.shape[3]
    shaped = adjoint.reshape(adjoint.shape[:3] + (WIDTH // cells, cells, RHS))
    dotted = jnp.sum(velocity[..., None] * shaped[:, :, :, 0:3], axis=3)
    slope = -0.11 / ((0.1 + design) * (0.1 + design))
    sensitivity = (mask.astype(f32) * slope)[..., None] * dotted
    return (adjoint, hessenberg, sensitivity)


def solution(mesh):
    shape = mesh.shape
    in_specs = (
        P("gx", "gy", "gz", None, None),
        P("gx", "gy", "gz", None),
        P("gx", "gy", "gz", None, None),
        P("gx", "gy", "gz", None, None),
        P("gx", "gy", "gz", None),
        P("gx", "gy", "gz", None),
    )
    out_specs = (P("gx", "gy", "gz", None, None), P(), P("gx", "gy", "gz", None, None))
    return jax.shard_map(
        functools.partial(per_device, shape["gx"], shape["gy"], shape["gz"]),
        mesh=mesh,
        in_specs=in_specs,
        out_specs=out_specs,
        check_vma=False,
    )
```
